128 devices in a mesh: grp: 16 (over x_hi, z, core), tp: 8 (over x_lo, y).
Axes of the slice: x: 4 (x_hi: 2, x_lo: 2; x = x_hi * 2 + x_lo), y: 4, z: 4, core: 2. Of those that a mesh axis runs over, the one named last changes fastest.
Arguments:
- hidden: bfloat16 [14336, 14336], P('grp', 'tp'), may hold values from -6 to 6
- frozen_down_matrix: bfloat16 [14336, 4096], P('tp'), may hold values from -0.046875 to 0.046875
- cotangent: bfloat16 [14336, 4096], P('grp', 'tp'), may hold values from -6 to 6
- adapter_input_maps: float32 [16, 64, 14336], P('grp', None, 'tp'), may hold values from -0.046875 to 0.046875
- adapter_output_maps: float32 [16, 64, 4096], P('grp', None, 'tp'), may hold values from -0.3 to 0.3
- input_first_moment: float32 [16, 64, 14336], P('grp', None, 'tp'), may hold values from -0.06 to 0.06
- input_second_moment: float32 [16, 64, 14336], P('grp', None, 'tp'), may hold values from 1e-06 to 0.0001
- output_first_moment: float32 [16, 64, 4096], P('grp', None, 'tp'), may hold values from -0.024 to 0.024
- output_second_moment: float32 [16, 64, 4096], P('grp', None, 'tp'), may hold values from 1e-07 to 1e-05
- group_adapter_list: int32 [16, 4], P('grp'), may hold values from 0 to 15, all different within a row
- token_adapter_slot: int32 [14336], P('grp'), may hold values from -1 to 3, as said below
Outputs:
- output: bfloat16 [14336, 4096], P('grp', 'tp')
- hidden_gradient: bfloat16 [14336, 14336], P('grp', 'tp')
- updated_input_maps: float32 [16, 64, 14336], P('grp', None, 'tp')
- updated_output_maps: float32 [16, 64, 4096], P('grp', None, 'tp')
- updated_input_first_moment: float32 [16, 64, 14336], P('grp', None, 'tp')
- updated_input_second_moment: float32 [16, 64, 14336], P('grp', None, 'tp')
- updated_output_first_moment: float32 [16, 64, 4096], P('grp', None, 'tp')
- updated_output_second_moment: float32 [16, 64, 4096], P('grp', None, 'tp')
The draws below stay inside these ranges and needn't reach their ends.
Inputs may be any that keep to these rules, and one draw needn't show every extreme that they name: `group_adapter_list`: each group's row names 4 different adapters; every adapter is named by some group. `token_adapter_slot`: within each group's 896 rows, a first run of at least 4 segments of 128 rows each holds one slot in a leading run of one or more rows and -1 in the rest; the later segments hold only -1; each slot 0 .. 3 appears in every group.
All inputs are finite; a program needn't handle non-finite values.
Results may differ from the reference program's by a relative error of at most 0.019.
Values may be sent and summed in bfloat16 or wider, within the bound.
A program may use at most 192 MiB of HBM per device.

```python
import math
import jax
import jax.numpy as jnp
from jax import lax

MODEL_WIDTH = 4096
HIDDEN_UNITS = 14336
ADAPTER_RANK = 64
SEG = 128
SEGS = 7
USE = 4
STEP = 20
FF_TP = 1792
ROW_TOTAL = 14336
ADAPTER_TOTAL = 16
N_GRP = 16
N_TP = 8


def draw_token_adapter_slot(key, part):
    key = jax.random.fold_in(key, 7)
    key_count, key_first, key_extra, key_rows = jax.random.split(key, 4)
    live_segments = jax.random.randint(key_count, (N_GRP,), USE, SEGS + 1)
    first_slots = jax.vmap(lambda k: jax.random.permutation(k, USE))(jax.random.split(key_first, N_GRP)).astype(jnp.int32)
    first_slots = jnp.concatenate([first_slots, jnp.zeros((N_GRP, SEGS - USE), jnp.int32)], axis=1)
    extra_slots = jax.random.randint(key_extra, (N_GRP, SEGS), 0, USE).astype(jnp.int32)
    segment_index = jnp.arange(SEGS)
    slots = jnp.where(segment_index[None, :] < USE, first_slots, extra_slots)
    rows_live = jax.random.randint(key_rows, (N_GRP, SEGS), 1, SEG + 1)
    last_live = live_segments - 1
    rows_live = jnp.where(segment_index[None, :] == last_live[:, None], jnp.minimum(rows_live, SEG - 1), rows_live)
    rows_live = jnp.where(segment_index[None, :] < live_segments[:, None], rows_live, 0)
    row_index = jnp.arange(SEG)
    slot_rows = jnp.where(row_index[None, None, :] < rows_live[:, :, None], slots[:, :, None], -1)
    return slot_rows.reshape(N_GRP * SEGS * SEG).astype(jnp.int32)


def level_of(own_key, dims, cuts, least, largest):
    level, own = 1.0, jax.random.fold_in(own_key, 6)
    for position, parts in cuts:
        heights = jnp.exp(jax.random.uniform(jax.random.fold_in(own, position), (parts,), jnp.float32, least / len(cuts), largest / len(cuts)))
        level = level * jnp.repeat(heights, dims[position] // parts).reshape([-1 if axis == position else 1 for axis in range(len(dims))])
    return level


def distinct(stream_key, rows, amount, top, lift):
    order = jax.random.permutation(jax.random.fold_in(stream_key, 1), amount)
    boost = order
    for power in range(3):
        boost = boost * boost // amount
    boost = boost * lift // amount
    chance = jax.random.randint(jax.random.fold_in(stream_key, 2), (rows, amount), 0, 4096) + boost
    holders = jax.random.permutation(jax.random.fold_in(stream_key, 3), rows)[jnp.arange(amount) % rows]
    chance = jnp.where(jnp.arange(rows)[:, None] == holders[None, :], 1 << 14, chance)
    priority = chance * amount + jnp.arange(amount)
    return lax.top_k(priority.astype(jnp.int32), top)[1].astype(jnp.int32)


def noise(rng, shape, spread, bound, pieces=(), kind=jnp.bfloat16):
    gain = level_of(rng, shape, pieces, -0.22, 0.18) if pieces else 1.0
    values = jax.random.normal(rng, shape, jnp.float32) * spread * gain
    return jnp.minimum(jnp.maximum(values, -bound), bound).astype(kind)


def setup_inputs(seed: int = 0) -> dict:
    seeds = jax.random.split(jax.random.key(seed), 12)
    hidden = noise(seeds[0], (ROW_TOTAL, HIDDEN_UNITS), 1.0, 6.0, ((0, 16), (1, 8)))
    frozen_down_matrix = noise(seeds[1], (HIDDEN_UNITS, MODEL_WIDTH), HIDDEN_UNITS ** -0.5, 0.046875, ((0, 8),))
    cotangent = noise(seeds[2], (ROW_TOTAL, MODEL_WIDTH), 1.0, 6.0, ((0, 16), (1, 8)))
    adapter_input_maps = noise(seeds[3], (ADAPTER_TOTAL, ADAPTER_RANK, HIDDEN_UNITS), HIDDEN_UNITS ** -0.5, 0.046875, ((0, 16), (2, 8)), jnp.float32)
    adapter_output_maps = noise(seeds[4], (ADAPTER_TOTAL, ADAPTER_RANK, MODEL_WIDTH), 0.05, 0.3, ((0, 16), (2, 8)), jnp.float32)
    input_first_moment = noise(seeds[5], (ADAPTER_TOTAL, ADAPTER_RANK, HIDDEN_UNITS), 0.01, 0.06, ((0, 16), (2, 8)), jnp.float32)
    input_second_moment = jnp.clip(jnp.exp(math.log(0.0001) - 4.6051702 * jax.random.uniform(seeds[6], (ADAPTER_TOTAL, ADAPTER_RANK, HIDDEN_UNITS), jnp.float32) ** level_of(seeds[6], (ADAPTER_TOTAL, ADAPTER_RANK, HIDDEN_UNITS), ((0, 16), (2, 8)), -0.2, 0.2)), 9.999999974752427e-07, 0.0001)
    output_first_moment = noise(seeds[7], (ADAPTER_TOTAL, ADAPTER_RANK, MODEL_WIDTH), 0.004, 0.024, ((0, 16), (2, 8)), jnp.float32)
    output_second_moment = jnp.clip(jnp.exp(math.log(9.999999747378752e-06) - 4.6051701 * jax.random.uniform(seeds[8], (ADAPTER_TOTAL, ADAPTER_RANK, MODEL_WIDTH), jnp.float32) ** level_of(seeds[8], (ADAPTER_TOTAL, ADAPTER_RANK, MODEL_WIDTH), ((0, 16), (2, 8)), -0.2, 0.2)), 1.0000000116860974e-07, 9.999999747378752e-06)
    group_adapter_list = distinct(seeds[9], N_GRP, ADAPTER_TOTAL, USE, 4096)
    token_adapter_slot = draw_token_adapter_slot(jax.random.fold_in(seeds[11], 71), 0)
    return {"hidden": hidden, "frozen_down_matrix": frozen_down_matrix, "cotangent": cotangent, "adapter_input_maps": adapter_input_maps, "adapter_output_maps": adapter_output_maps, "input_first_moment": input_first_moment, "input_second_moment": input_second_moment, "output_first_moment": output_first_moment, "output_second_moment": output_second_moment, "group_adapter_list": group_adapter_list, "token_adapter_slot": token_adapter_slot}


ADAPTER_SCALE = 2.0
LEARN_RATE = 0.001
BETA_ONE = 0.9
BETA_TWO = 0.999
ADAM_EPS = 1e-08

def moment_optimizer_step(param, moment, second, grad):
    new_moment = BETA_ONE * moment + (1.0 - BETA_ONE) * grad
    new_second = BETA_TWO * second + (1.0 - BETA_TWO) * grad * grad
    fix_one = 1.0 - BETA_ONE ** STEP
    fix_two = 1.0 - BETA_TWO ** STEP
    new_param = param - LEARN_RATE * (new_moment / fix_one) / (jnp.sqrt(new_second / fix_two) + ADAM_EPS)
    return (new_param, new_moment, new_second)

def reference(hidden, frozen_down_matrix, cotangent, adapter_input_maps, adapter_output_maps, input_first_moment, input_second_moment, output_first_moment, output_second_moment, group_adapter_list, token_adapter_slot):
    segment_count = N_GRP * SEGS
    segment_slot = token_adapter_slot.reshape(segment_count, SEG)[:, 0]
    segment_group = jnp.arange(segment_count).astype(jnp.int32) // SEGS
    piece_adapter_index = group_adapter_list[segment_group, jnp.maximum(segment_slot, 0)]
    valid_mask = (token_adapter_slot >= 0).astype(jnp.float32).reshape(segment_count, SEG, 1)
    input_map_half = adapter_input_maps.astype(jnp.bfloat16)
    output_map_half = adapter_output_maps.astype(jnp.bfloat16)
    hidden_pieces = hidden.reshape(segment_count, SEG, HIDDEN_UNITS)
    upstream_gradient_pieces = cotangent.reshape(segment_count, SEG, MODEL_WIDTH)

    def segment_piece(carry, items):
        input_map_gradient, output_map_gradient = carry
        hidden_row_block, upstream_gradient_rows, valid_row_mask, adapter_entry = items
        input_map_rows = input_map_half[adapter_entry]
        output_map_rows = output_map_half[adapter_entry]
        adapter_input_product = (valid_row_mask * jnp.dot(hidden_row_block, input_map_rows.T, preferred_element_type=jnp.float32)).astype(jnp.bfloat16)
        adapter_gradient_path = (valid_row_mask * jnp.dot(upstream_gradient_rows, output_map_rows.T, preferred_element_type=jnp.float32)).astype(jnp.bfloat16)
        adapter_output_product = jnp.dot(adapter_input_product, output_map_rows, preferred_element_type=jnp.float32)
        adapter_hidden_gradient = jnp.dot(adapter_gradient_path, input_map_rows, preferred_element_type=jnp.float32)
        input_map_gradient = input_map_gradient.at[adapter_entry].add(jnp.dot(adapter_gradient_path.T, hidden_row_block, preferred_element_type=jnp.float32))
        output_map_gradient = output_map_gradient.at[adapter_entry].add(jnp.dot(adapter_input_product.T, upstream_gradient_rows, preferred_element_type=jnp.float32))
        return ((input_map_gradient, output_map_gradient), (adapter_output_product, adapter_hidden_gradient))
    initial_gradients = (jnp.zeros((ADAPTER_TOTAL, ADAPTER_RANK, HIDDEN_UNITS), jnp.float32), jnp.zeros((ADAPTER_TOTAL, ADAPTER_RANK, MODEL_WIDTH), jnp.float32))
    (input_map_gradient, output_map_gradient), (adapter_output_product, adapter_hidden_gradient) = lax.scan(segment_piece, initial_gradients, (hidden_pieces, upstream_gradient_pieces, valid_mask, piece_adapter_index))
    input_map_gradient = input_map_gradient * (ADAPTER_SCALE / ROW_TOTAL)
    output_map_gradient = output_map_gradient * (ADAPTER_SCALE / ROW_TOTAL)
    frozen_output = jnp.zeros((ROW_TOTAL, MODEL_WIDTH), jnp.float32)
    for block in range(N_TP):
        product = jnp.dot(hidden[:, block * FF_TP:(block + 1) * FF_TP], frozen_down_matrix[block * FF_TP:(block + 1) * FF_TP], preferred_element_type=jnp.float32)
        frozen_output = frozen_output + lax.optimization_barrier(product.astype(jnp.bfloat16)).astype(jnp.float32)
    output = (frozen_output + ADAPTER_SCALE * adapter_output_product.reshape(ROW_TOTAL, MODEL_WIDTH)).astype(jnp.bfloat16)
    frozen_gradient_path = jnp.dot(cotangent, frozen_down_matrix.T, preferred_element_type=jnp.float32)
    hidden_gradient = (frozen_gradient_path + ADAPTER_SCALE * adapter_hidden_gradient.reshape(ROW_TOTAL, HIDDEN_UNITS)).astype(jnp.bfloat16)
    updated_input_maps, updated_input_first_moment, updated_input_second_moment = moment_optimizer_step(adapter_input_maps, input_first_moment, input_second_moment, input_map_gradient)
    updated_output_maps, updated_output_first_moment, updated_output_second_moment = moment_optimizer_step(adapter_output_maps, output_first_moment, output_second_moment, output_map_gradient)
    return (output, hidden_gradient, updated_input_maps, updated_output_maps, updated_input_first_moment, updated_input_second_moment, updated_output_first_moment, updated_output_second_moment)
```

```python
import functools

import jax
import jax.numpy as jnp
from jax import lax
from jax.experimental import pallas as pl
from jax.experimental.pallas import tpu as pltpu
from jax.sharding import PartitionSpec as P

MESH = pl.DeviceIdType.MESH
BF = jnp.bfloat16
F32 = jnp.float32

SEG = 128
HALF = 64
SEGS = 7
USE = 4
STEP = 20
RANK = 64
WIDE = USE * RANK
NY = 4
NZ = 4
P_SEGS = (0, 1, 2)
Q_SEGS = (3, 4, 5, 6)
ORDER = (3, 0, 4, 1, 5, 2, 6)

ADAPTER_SCALE = 2.0
LEARN_RATE = 0.001
BETA_ONE = 0.9
BETA_TWO = 0.999
ADAM_EPS = 1e-08


def moment_optimizer_step(param, moment, second, grad):
    new_moment = BETA_ONE * moment + (1.0 - BETA_ONE) * grad
    new_second = BETA_TWO * second + (1.0 - BETA_TWO) * grad * grad
    fix_one = 1.0 - BETA_ONE**STEP
    fix_two = 1.0 - BETA_TWO**STEP
    new_param = param - LEARN_RATE * (new_moment / fix_one) / (
        jnp.sqrt(new_second / fix_two) + ADAM_EPS
    )
    return (new_param, new_moment, new_second)


def nt_dot(a, b):
    return lax.dot_general(a, b, (((1,), (1,)), ((), ())), preferred_element_type=F32)


def tn_dot(a, b):
    return lax.dot_general(a, b, (((0,), (0,)), ((), ())), preferred_element_type=F32)


def nn_dot(a, b):
    return jnp.dot(a, b, preferred_element_type=F32)


G_X, G_U, G_D, G_XU, G_XD, G_O0, G_O1, G_XO0, G_XO1 = range(9)
R_F0, R_F1, R_D0, R_D1, R_U0, R_U1, R_X = range(7)
M_X, M_U, M_D, M_XU, M_XD, M_O, M_XO = range(7)
S_F0, S_F1, S_D0, S_D1, S_U0, S_U1, S_X = range(4, 11)


def kernel(
    grad_scale,
    hid,
    w,
    cot,
    amap,
    bmap,
    lst,
    slots,
    out,
    hgrad,
    gsum,
    wv,
    hv,
    cotf,
    part,
    qf0,
    qf1,
    qru,
    qrd,
    qx,
    pf0,
    pf1,
    pru,
    prd,
    px,
    am32,
    bm32,
    aall,
    acat,
    mask,
    rk,
    rr,
    tot,
    lix,
    lbx,
    gslot,
    con,
    sb,
    gf,
    grd,
    gru,
    gx,
    gtot,
    outv,
    ld_sem,
    w_sem,
    st_sem,
    g_ss,
    g_rs,
    r_ss,
    r_rs,
    k_ss,
    k_rs,
    m_ss,
    m_rs,
    b_ss,
    b_rs,
    s_ss,
    s_rs,
):
    feat = cot.shape[1]
    units = hid.shape[1]
    rows_n = hid.shape[0]
    me = lax.axis_index("tp")
    xl, y = lax.div(me, NY), lax.rem(me, NY)
    ox = 1 - xl
    yu, yd, yo = lax.rem(y + 1, NY), lax.rem(y + 3, NY), lax.rem(y + 2, NY)
    t_x, t_u, t_d, t_o = ox * NY + y, xl * NY + yu, xl * NY + yd, xl * NY + yo
    t_xu, t_xd, t_xo = ox * NY + yu, ox * NY + yd, ox * NY + yo
    g = lax.axis_index("grp")
    xh, z, core = lax.div(g, 2 * NZ), lax.rem(lax.div(g, 2), NZ), lax.rem(g, 2)
    zu, zd, zo = lax.rem(z + 1, NZ), lax.rem(z + 3, NZ), lax.rem(z + 2, NZ)
    oxh = 1 - xh

    def grp_id(a, b, c):
        return a * (2 * NZ) + b * 2 + c

    n_x, n_u, n_d = grp_id(oxh, z, core), grp_id(xh, zu, core), grp_id(xh, zd, core)
    n_s = grp_id(xh, z, 1 - core)

    def col(k):
        return pl.ds(pl.multiple_of(k * feat, 128), feat)

    def seg(s):
        return pl.ds(s * SEG, SEG)

    def half(s, h):
        return pl.ds(s * SEG + h * HALF, HALF)

    ld_a = pltpu.make_async_copy(amap, am32, ld_sem.at[0])
    ld_b = pltpu.make_async_copy(bmap, bm32, ld_sem.at[1])
    ld_h = pltpu.make_async_copy(hid, hv, ld_sem.at[2])
    ld_c = pltpu.make_async_copy(cot, cotf.at[:, col(me)], ld_sem.at[3])
    ld_a.start()
    ld_b.start()
    ld_h.start()
    blocks = [(yq, c) for yq in (yo, yu, yd, y) for c in (0, 1)]
    ld_w = []
    for i, (yq, c) in enumerate(blocks):
        k = c * NY + yq
        ld_w.append(pltpu.make_async_copy(w.at[:, col(k)], wv.at[:, col(k)], w_sem.at[i]))
        ld_w[-1].start()
    ld_c.start()

    barrier = pltpu.get_barrier_semaphore()
    for i in range(1, 2 * NY):
        pl.semaphore_signal(
            barrier, inc=1, device_id={"tp": lax.rem(me + i, 2 * NY)}, device_id_type=MESH
        )
    for dev in (n_x, n_u, n_d, n_s):
        pl.semaphore_signal(barrier, inc=1, device_id={"grp": dev}, device_id_type=MESH)

    ld_a.wait()
    ld_b.wait()
    aall[g, :, pl.ds(0, units)] = am32[...].astype(BF)
    aall[g, :, pl.ds(units, feat)] = bm32[...].astype(BF)

    pl.semaphore_wait(barrier, 2 * NY - 1 + 4)

    sends = []

    def push(src, dst, ss, rs, axis, dev):
        c = pltpu.make_async_remote_copy(
            src_ref=src,
            dst_ref=dst,
            send_sem=ss,
            recv_sem=rs,
            device_id={axis: dev},
            device_id_type=MESH,
        )
        c.start()
        sends.append(c)

    def arrived(dst, ss, rs, axis):
        pltpu.make_async_remote_copy(
            src_ref=dst,
            dst_ref=dst,
            send_sem=ss,
            recv_sem=rs,
            device_id={axis: me if axis == "tp" else g},
            device_id_type=MESH,
        ).wait_recv()

    def g_push(slot, s, rows, k, dev, src=None):
        ref = cotf.at[rows, col(k)]
        push(ref if src is None else src, ref, g_ss.at[slot, s], g_rs.at[slot, s], "tp", dev)

    def g_wait(slot, s, rows, k):
        arrived(cotf.at[rows, col(k)], g_ss.at[slot, s], g_rs.at[slot, s], "tp")

    def gather_start(s):
        own = cot.at[seg(s), :]
        g_push(G_X, s, seg(s), me, t_x, own)
        g_push(G_D, s, seg(s), me, t_u, own)
        g_push(G_U, s, seg(s), me, t_d, own)

    def gather_one(s):
        if s in Q_SEGS:
            g_wait(G_X, s, seg(s), t_x)
            g_push(G_XD, s, seg(s), t_x, t_u)
            g_push(G_XU, s, seg(s), t_x, t_d)
            g_wait(G_D, s, seg(s), t_d)
            g_push(G_O0, s, half(s, 0), t_d, t_u)
            g_wait(G_U, s, seg(s), t_u)
            g_push(G_O1, s, half(s, 1), t_u, t_d)
        else:
            g_wait(G_D, s, seg(s), t_d)
            g_push(G_O0, s, half(s, 0), t_d, t_u)
            g_push(G_XD, s, seg(s), t_d, t_x)
            g_wait(G_U, s, seg(s), t_u)
            g_push(G_O1, s, half(s, 1), t_u, t_d)
            g_push(G_XU, s, seg(s), t_u, t_x)
            g_wait(G_X, s, seg(s), t_x)

    def gather_two(s):
        if s in Q_SEGS:
            g_wait(G_XD, s, seg(s), t_xd)
            g_push(G_XO0, s, half(s, 0), t_xd, t_u)
            g_wait(G_XU, s, seg(s), t_xu)
            g_push(G_XO1, s, half(s, 1), t_xu, t_d)
            g_wait(G_O0, s, half(s, 0), t_o)
            g_wait(G_O1, s, half(s, 1), t_o)
        else:
            g_wait(G_O0, s, half(s, 0), t_o)
            g_push(G_XO0, s, half(s, 0), t_o, t_x)
            g_wait(G_O1, s, half(s, 1), t_o)
            g_push(G_XO1, s, half(s, 1), t_o, t_x)
            g_wait(G_XD, s, seg(s), t_xd)
            g_wait(G_XU, s, seg(s), t_xu)

    def gather_end(s):
        g_wait(G_XO0, s, half(s, 0), t_xo)
        g_wait(G_XO1, s, half(s, 1), t_xo)

    def m_push(slot, o, dev):
        push(aall.at[o], aall.at[o], m_ss.at[slot], m_rs.at[slot], "grp", dev)

    def m_wait(slot, o):
        arrived(aall.at[o], m_ss.at[slot], m_rs.at[slot], "grp")

    def b_push(i, o):
        push(aall.at[o], aall.at[o], b_ss.at[i], b_rs.at[i], "grp", n_s)

    def maps_start():
        m_push(M_X, g, n_x)
        m_push(M_D, g, n_u)
        m_push(M_U, g, n_d)
        b_push(7, g)

    def maps_one():
        m_wait(M_X, n_x)
        m_push(M_XD, n_x, n_u)
        m_push(M_XU, n_x, n_d)
        b_push(M_X, n_x)
        m_wait(M_D, n_d)
        m_push(M_O, n_d, n_u)
        b_push(M_D, n_d)
        m_wait(M_U, n_u)
        b_push(M_U, n_u)

    def maps_two():
        m_wait(M_XU, grp_id(oxh, zu, core))
        m_push(M_XO, grp_id(oxh, zu, core), n_d)
        b_push(M_XU, grp_id(oxh, zu, core))
        m_wait(M_XD, grp_id(oxh, zd, core))
        b_push(M_XD, grp_id(oxh, zd, core))
        m_wait(M_O, grp_id(xh, zo, core))
        b_push(M_O, grp_id(xh, zo, core))

    def maps_end():
        m_wait(M_XO, grp_id(oxh, zo, core))
        b_push(M_XO, grp_id(oxh, zo, core))
        sib = 1 - core
        for i, o in (
            (7, grp_id(xh, z, sib)),
            (M_X, grp_id(oxh, z, sib)),
            (M_D, grp_id(xh, zd, sib)),
            (M_U, grp_id(xh, zu, sib)),
            (M_XU, grp_id(oxh, zu, sib)),
            (M_XD, grp_id(oxh, zd, sib)),
            (M_O, grp_id(xh, zo, sib)),
            (M_XO, grp_id(oxh, zo, sib)),
        ):
            arrived(aall.at[o], b_ss.at[i], b_rs.at[i], "grp")

    def part_block(i):
        yq, c = blocks[i]
        k = c * NY + yq
        ld_w[i].wait()
        step = feat // 2

        @pl.loop(0, 2)
        def _(j):
            wt = wv[:, pl.ds(pl.multiple_of(k * feat + j * step, 128), step)]
            at = pl.ds(pl.multiple_of(c * feat + j * step, 128), step)
            part[yq, :, at] = nn_dot(hv[...], wt).astype(BF)

    def r_push(src, dst, slot, s, dev):
        push(src, dst, r_ss.at[slot, s], r_rs.at[slot, s], "tp", dev)

    def r_wait(dst, slot, s):
        arrived(dst, r_ss.at[slot, s], r_rs.at[slot, s], "tp")

    def bufs(s):
        if s in Q_SEGS:
            i = s - Q_SEGS[0]
            return qf0.at[i], qf1.at[i], qru.at[i], qrd.at[i], pl.ds(0, 2 * feat)
        i = s - P_SEGS[0]
        return pf0.at[i], pf1.at[i], pru.at[i], prd.at[i], col(xl)

    h0, h1 = pl.ds(0, HALF), pl.ds(HALF, HALF)

    def y_sends(s):
        f0, f1, ru, rd, cs = bufs(s)
        r_push(part.at[yo, half(s, 0), cs], f0, R_F0, s, t_u)
        r_push(part.at[yo, half(s, 1), cs], f1, R_F1, s, t_d)
        r_push(part.at[yu, half(s, 1), cs], rd.at[h1, :], R_D1, s, t_u)
        r_push(part.at[yd, half(s, 0), cs], ru.at[h0, :], R_U0, s, t_d)

    def add_into(ref, idx, other):
        ref[idx] = (ref[idx].astype(F32) + other.astype(F32)).astype(BF)

    def scatter_start(s):
        if s in Q_SEGS:
            y_sends(s)
        else:
            r_push(part.at[:, seg(s), col(ox)], px.at[s - P_SEGS[0]], R_X, s, t_x)

    def scatter_x(s):
        i = s - P_SEGS[0]
        r_wait(px.at[i], R_X, s)
        for yq in (yo, yu, yd):
            add_into(part, (yq, seg(s), col(xl)), px[i, yq])
        y_sends(s)

    def scatter_mid(s):
        f0, f1, ru, rd, cs = bufs(s)
        r_wait(f0, R_F0, s)
        add_into(part, (yu, half(s, 0), cs), f0[...])
        r_push(part.at[yu, half(s, 0), cs], rd.at[h0, :], R_D0, s, t_u)
        r_wait(f1, R_F1, s)
        add_into(part, (yd, half(s, 1), cs), f1[...])
        r_push(part.at[yd, half(s, 1), cs], ru.at[h1, :], R_U1, s, t_d)

    def scatter_y(s):
        _, _, ru, rd, _ = bufs(s)
        r_wait(rd.at[h1, :], R_D1, s)
        r_wait(ru.at[h0, :], R_U0, s)
        r_wait(rd.at[h0, :], R_D0, s)
        r_wait(ru.at[h1, :], R_U1, s)
        if s in Q_SEGS:
            i = s - Q_SEGS[0]
            cs = col(ox)
            total = (
                part[y, seg(s), cs].astype(F32)
                + qru[i, :, cs].astype(F32)
                + qrd[i, :, cs].astype(F32)
            )
            part[y, seg(s), cs] = total.astype(BF)
            r_push(part.at[y, seg(s), cs], qx.at[i], R_X, s, t_x)

    def scatter_end(s):
        cs = col(xl)
        if s in Q_SEGS:
            i = s - Q_SEGS[0]
            r_wait(qx.at[i], R_X, s)
            total = (
                part[y, seg(s), cs].astype(F32)
                + qru[i, :, cs].astype(F32)
                + qrd[i, :, cs].astype(F32)
                + qx[i].astype(F32)
            )
        else:
            i = s - P_SEGS[0]
            total = (
                part[y, seg(s), cs].astype(F32)
                + px[i, y].astype(F32)
                + pru[i].astype(F32)
                + prd[i].astype(F32)
            )
        lora = nn_dot(lix[seg(s), :], acat[:, pl.ds(units, feat)])
        outv[seg(s), :] = (total + ADAPTER_SCALE * lora).astype(BF)
        c = pltpu.make_async_copy(outv.at[seg(s), :], out.at[seg(s), :], st_sem.at[s])
        c.start()
        stores.append(c)

    stores = []

    def build_mask():
        lane = lax.broadcasted_iota(jnp.int32, (SEG, WIDE), 1)
        unit = lax.shift_right_logical(lane, 6).astype(F32)
        for s in range(SEGS):
            line = jnp.broadcast_to(slots[pl.ds(s, 1), :].astype(F32), (SEG, SEG))
            wide = jnp.concatenate([line.T] * (WIDE // SEG), axis=1)
            mask[seg(s), :] = jnp.where(wide == unit, 1.0, 0.0).astype(BF)

    def pick(shape, dim, shift):
        i = jnp.bitwise_and(lax.broadcasted_iota(jnp.int32, shape, dim), RANK - 1)
        j = lax.broadcasted_iota(jnp.int32, shape, 1 - dim)
        return jnp.where(i + shift == j, 1.0, 0.0).astype(BF)

    def rank_start():
        for u in range(USE):
            acat[pl.ds(u * RANK, RANK), :] = aall[lst[0, u]]
        m = mask[...].astype(F32)
        down = (nt_dot(hv[...], acat[:, pl.ds(0, units)]) * m).astype(BF)
        back = (nt_dot(cotf[:, col(me)], acat[:, pl.ds(units, feat)]) * m).astype(BF)
        rk[...] = (
            nn_dot(down, pick((WIDE, 2 * RANK), 0, 0))
            + nn_dot(back, pick((WIDE, 2 * RANK), 0, RANK))
        ).astype(BF)
        n = rows_n // (2 * NY)
        for i in range(1, 2 * NY):
            dev = lax.rem(me + i, 2 * NY)
            src = rk.at[pl.ds(pl.multiple_of(dev * n, 16), n), :]
            push(src, rr.at[i], k_ss.at[0, i], k_rs.at[0, i], "tp", dev)

    def rank_sum():
        n = rows_n // (2 * NY)
        mine = pl.ds(pl.multiple_of(me * n, 16), n)
        total = rk[mine, :].astype(F32)
        for i in range(1, 2 * NY):
            arrived(rr.at[i], k_ss.at[0, i], k_rs.at[0, i], "tp")
            total = total + rr[i].astype(F32)
        tot[mine, :] = total.astype(BF)
        for i in range(1, 2 * NY):
            dev = lax.rem(me + i, 2 * NY)
            push(tot.at[mine, :], tot.at[mine, :], k_ss.at[1, i], k_rs.at[1, i], "tp", dev)

    def rank_end():
        n = rows_n // (2 * NY)
        for i in range(1, 2 * NY):
            src = lax.rem(me + 2 * NY - i, 2 * NY)
            theirs = pl.ds(pl.multiple_of(src * n, 16), n)
            arrived(tot.at[theirs, :], k_ss.at[1, i], k_rs.at[1, i], "tp")
        m = mask[...].astype(F32)
        lix[...] = (nn_dot(tot[...], pick((2 * RANK, WIDE), 1, 0)) * m).astype(BF)
        lbx[...] = (nn_dot(tot[...], pick((2 * RANK, WIDE), 1, RANK)) * m).astype(BF)

    def grads():
        step = 256
        wide = units + feat

        @pl.loop(0, units // step)
        def _(j):
            at = pl.ds(pl.multiple_of(j * step, 128), step)
            ga = tn_dot(lbx[...], hv[:, at]) * grad_scale
            for u in range(USE):
                gslot[u, :, at] = ga[u * RANK : (u + 1) * RANK, :].astype(BF)

        gb = tn_dot(lix[...], cotf[:, col(me)]) * grad_scale
        for u in range(USE):
            gslot[u, :, pl.ds(units, feat)] = gb[u * RANK : (u + 1) * RANK, :].astype(BF)
        gslot[USE] = jnp.zeros((RANK, wide), BF)
        for o in range(4 * NZ):
            at = jnp.int32(USE)
            for u in range(USE):
                at = jnp.where(lst[0, u] == o, u, at)
            con[o % 2, (o // 2) % NZ, o // (2 * NZ)] = gslot[at]

    def s_push(src, dst, slot, dev):
        push(src, dst, s_ss.at[slot], s_rs.at[slot], "grp", dev)

    def s_wait(dst, slot):
        arrived(dst, s_ss.at[slot], s_rs.at[slot], "grp")

    def sum_start():
        for i, zq in enumerate((zo, zu, zd, z)):
            s_push(con.at[1 - core, zq], sb.at[zq], i, n_s)

    def sum_one():
        s_wait(sb.at[zo], 0)
        add_into(con, (core, zo), sb[zo])
        s_push(con.at[core, zo, 0], gf.at[0], S_F0, n_u)
        s_push(con.at[core, zo, 1], gf.at[1], S_F1, n_d)
        s_wait(sb.at[zu], 1)
        add_into(con, (core, zu), sb[zu])
        s_push(con.at[core, zu, 1], grd.at[1], S_D1, n_u)
        s_wait(sb.at[zd], 2)
        add_into(con, (core, zd), sb[zd])
        s_push(con.at[core, zd, 0], gru.at[0], S_U0, n_d)
        s_wait(sb.at[z], 3)

    def sum_mid():
        s_wait(gf.at[0], S_F0)
        add_into(con, (core, zu, 0), gf[0])
        s_push(con.at[core, zu, 0], grd.at[0], S_D0, n_u)
        s_wait(gf.at[1], S_F1)
        add_into(con, (core, zd, 1), gf[1])
        s_push(con.at[core, zd, 1], gru.at[1], S_U1, n_d)

    def sum_total(h):
        return (
            con[core, z, h].astype(F32)
            + sb[z, h].astype(F32)
            + grd[h].astype(F32)
            + gru[h].astype(F32)
        )

    def sum_x():
        s_wait(grd.at[1], S_D1)
        s_wait(gru.at[0], S_U0)
        s_wait(grd.at[0], S_D0)
        s_wait(gru.at[1], S_U1)
        con[core, z, oxh] = sum_total(oxh).astype(BF)
        s_push(con.at[core, z, oxh], gx, S_X, n_x)

    def sum_end():
        s_wait(gx, S_X)
        gtot[...] = sum_total(xh) + gx[...].astype(F32)
        c = pltpu.make_async_copy(gtot, gsum, st_sem.at[SEGS])
        c.start()
        stores.append(c)

    step = 256
    tiles = units // step

    def hidden_tile(j):
        at = pl.ds(j * step, step)
        r = nt_dot(cotf[...], wv[at, :]) + ADAPTER_SCALE * nn_dot(lbx[...], acat[:, at])
        hv[:, at] = r.astype(BF)
        c = pltpu.make_async_copy(hv.at[:, at], hgrad.at[:, at], st_sem.at[SEGS + 1 + j])
        c.start()
        stores.append(c)

    maps_start()
    for s in ORDER:
        gather_start(s)
    build_mask()
    ld_h.wait()
    part_block(0)
    part_block(1)
    gather_one(ORDER[0])
    part_block(2)
    gather_one(ORDER[1])
    part_block(3)
    maps_one()
    part_block(4)
    gather_one(ORDER[2])
    gather_two(ORDER[0])
    part_block(5)
    gather_one(ORDER[3])
    gather_two(ORDER[1])
    maps_two()
    part_block(6)
    gather_one(ORDER[4])
    gather_two(ORDER[2])
    part_block(7)
    gather_one(ORDER[5])
    gather_two(ORDER[3])
    maps_end()
    ld_c.wait()
    rank_start()
    gather_one(ORDER[6])
    gather_two(ORDER[4])
    for s in ORDER:
        scatter_start(s)
    gather_two(ORDER[5])
    rank_sum()
    gather_two(ORDER[6])
    for s in P_SEGS:
        scatter_x(s)
    rank_end()
    grads()
    sum_start()
    for s in ORDER:
        gather_end(s)
    scatter_mid(ORDER[0])
    sum_one()
    for i in range(6):
        hidden_tile(i)
        scatter_mid(ORDER[i + 1])
        if i == 3:
            sum_mid()
    hidden_tile(6)
    for s in Q_SEGS:
        scatter_y(s)
    sum_x()
    for s in P_SEGS:
        scatter_y(s)
        scatter_end(s)
    sum_end()
    for s in Q_SEGS:
        scatter_end(s)
    for c in sends:
        c.wait_send()
    for c in stores:
        c.wait()


def fused(hidden, w, cot, amap, bmap, lst, slots, rows_all):
    rows, units = hidden.shape
    feat = cot.shape[1]
    wide = units + feat
    nq, np_ = len(Q_SEGS), len(P_SEGS)
    any_ = pl.BlockSpec(memory_space=pl.ANY)
    dma = pltpu.SemaphoreType.DMA
    v = pltpu.VMEM
    return pl.pallas_call(
        functools.partial(kernel, ADAPTER_SCALE / rows_all),
        out_shape=(
            jax.ShapeDtypeStruct((rows, feat), BF),
            jax.ShapeDtypeStruct((rows, units), BF),
            jax.ShapeDtypeStruct((RANK, wide), F32),
        ),
        in_specs=[any_] * 5
        + [pl.BlockSpec(memory_space=pltpu.SMEM), pl.BlockSpec(memory_space=pltpu.VMEM)],
        out_specs=(any_, any_, any_),
        scratch_shapes=[
            v((units, 2 * NY * feat), BF),
            v((rows, units), BF),
            v((rows, 2 * NY * feat), BF),
            v((NY, rows, 2 * feat), BF),
            v((nq, HALF, 2 * feat), BF),
            v((nq, HALF, 2 * feat), BF),
            v((nq, SEG, 2 * feat), BF),
            v((nq, SEG, 2 * feat), BF),
            v((nq, SEG, feat), BF),
            v((np_, HALF, feat), BF),
            v((np_, HALF, feat), BF),
            v((np_, SEG, feat), BF),
            v((np_, SEG, feat), BF),
            v((np_, NY, SEG, feat), BF),
            v((RANK, units), F32),
            v((RANK, feat), F32),
            v((4 * NZ, RANK, wide), BF),
            v((WIDE, wide), BF),
            v((rows, WIDE), BF),
            v((rows, 2 * RANK), BF),
            v((2 * NY, rows // (2 * NY), 2 * RANK), BF),
            v((rows, 2 * RANK), BF),
            v((rows, WIDE), BF),
            v((rows, WIDE), BF),
            v((USE + 1, RANK, wide), BF),
            v((2, NZ, 2, RANK, wide), BF),
            v((NZ, 2, RANK, wide), BF),
            v((2, RANK, wide), BF),
            v((2, RANK, wide), BF),
            v((2, RANK, wide), BF),
            v((RANK, wide), BF),
            v((RANK, wide), F32),
            v((rows, feat), BF),
            dma((4,)),
            dma((2 * NY,)),
            dma((SEGS + 1 + units // 256,)),
            dma((9, SEGS)),
            dma((9, SEGS)),
            dma((7, SEGS)),
            dma((7, SEGS)),
            dma((2, 2 * NY)),
            dma((2, 2 * NY)),
            dma((7,)),
            dma((7,)),
            dma((8,)),
            dma((8,)),
            dma((11,)),
            dma((11,)),
        ],
        compiler_params=pltpu.CompilerParams(
            collective_id=0,
            has_side_effects=True,
            vmem_limit_bytes=64 * 1024 * 1024,
        ),
    )(hidden, w, cot, amap, bmap, lst, slots)


def per_device(
    hidden,
    frozen_down_matrix,
    cotangent,
    adapter_input_maps,
    adapter_output_maps,
    input_first_moment,
    input_second_moment,
    output_first_moment,
    output_second_moment,
    group_adapter_list,
    token_adapter_slot,
):
    units = hidden.shape[1]
    rows_all = hidden.shape[0] * lax.axis_size("grp")
    output, hidden_gradient, grad = fused(
        hidden,
        frozen_down_matrix,
        cotangent,
        adapter_input_maps[0],
        adapter_output_maps[0],
        group_adapter_list,
        token_adapter_slot.reshape(SEGS, SEG),
        rows_all,
    )
    new_a, new_a_m, new_a_v = moment_optimizer_step(
        adapter_input_maps, input_first_moment, input_second_moment, grad[None, :, :units]
    )
    new_b, new_b_m, new_b_v = moment_optimizer_step(
        adapter_output_maps, output_first_moment, output_second_moment, grad[None, :, units:]
    )
    return (output, hidden_gradient, new_a, new_b, new_a_m, new_a_v, new_b_m, new_b_v)


def solution(mesh):
    return jax.shard_map(
        per_device,
        mesh=mesh,
        in_specs=(
            P("grp", "tp"),
            P("tp", None),
            P("grp", "tp"),
            P("grp", None, "tp"),
            P("grp", None, "tp"),
            P("grp", None, "tp"),
            P("grp", None, "tp"),
            P("grp", None, "tp"),
            P("grp", None, "tp"),
            P("grp", None),
            P("grp"),
        ),
        out_specs=(
            P("grp", "tp"),
            P("grp", "tp"),
            P("grp", None, "tp"),
            P("grp", None, "tp"),
            P("grp", None, "tp"),
            P("grp", None, "tp"),
            P("grp", None, "tp"),
            P("grp", None, "tp"),
        ),
        check_vma=False,
    )
```

```python
import functools

import jax
import jax.numpy as jnp
from jax import lax
from jax.experimental import pallas as pl
from jax.experimental.pallas import tpu as pltpu
from jax.sharding import PartitionSpec as P

MESH = pl.DeviceIdType.MESH
BF = jnp.bfloat16
F32 = jnp.float32

SEG = 128
HALF = 64
SEGS = 7
USE = 4
STEP = 20
RANK = 64
WIDE = USE * RANK
NY = 4
NZ = 4
Y_FIRST = (0, 1, 2)
X_SUMS = (0, 1)
Y_SUMS = tuple(s for s in range(SEGS) if s not in X_SUMS)
CUT = 3 * SEG

ORDER = (
    ("gs_x", 5), ("gs_u", 2), ("gs_d", 2), ("m_start",), ("gs_d", 3),
    ("gs_u", 0), ("gs_x", 4), ("gs_u", 5), ("part", 0), ("gs_x", 3),
    ("part", 1), ("r_so", 5), ("gs_d", 0), ("gs_x", 1), ("part", 2),
    ("part", 3), ("r_xu", 1), ("g_d", 2), ("m_d",), ("g_d", 0),
    ("r_so", 2), ("m_x",), ("gs_u", 3), ("gs_d", 5), ("g_u", 0),
    ("r_su", 2), ("m_u",), ("gs_d", 1), ("gs_u", 4), ("part", 4),
    ("part", 5), ("r_sd", 6), ("g_d", 5), ("gs_u", 6), ("gs_u", 1),
    ("r_m1", 2), ("gs_x", 2), ("g_x", 5), ("m_o",), ("m_xu",),
    ("m_xd",), ("r_xd", 1), ("gs_x", 0), ("gs_d", 4), ("m_xo",),
    ("g_x", 4), ("gs_d", 6), ("m_end",), ("rank_start",), ("g_u", 2),
    ("g_d", 3), ("r_so", 6), ("g_u", 3), ("gs_x", 6), ("rank_sum",),
    ("g_d", 1), ("g_u", 1), ("g_o0", 0), ("part", 6), ("g_d", 4),
    ("g_xd", 5), ("g_u", 6), ("part", 7), ("g_o1", 0), ("r_su", 3),
    ("r_sd", 2), ("g_x", 6), ("g_o0", 1), ("g_o1", 2), ("g_u", 5),
    ("g_x", 3), ("r_su", 6), ("r_xm", 1), ("r_xo", 1), ("rank_end",),
    ("grads",), ("sum_start",), ("g_o1", 1), ("g_u", 4), ("r_m1", 6),
    ("r_xo", 0), ("s_o",), ("r_m0", 6), ("r_m0", 2), ("s_d",),
    ("g_o0", 2), ("r_so", 3), ("s_u",), ("g_end", 0), ("g_xd", 4),
    ("g_xu", 5), ("r_so", 4), ("g_xu", 4), ("r_sd", 5), ("g_xu", 3),
    ("r_ao", 1), ("g_d", 6), ("r_y", 2), ("r_xd", 0), ("g_xu", 6),
    ("r_m1", 3), ("r_y", 6), ("r_xm", 0), ("g_xd", 6), ("s_m1",),
    ("s_m0",), ("r_xu", 0), ("g_xd", 3), ("r_m0", 3), ("r_sd", 4),
    ("r_m0", 5), ("r_sd", 3), ("g_end", 2), ("g_end", 1), ("hidA", 0),
    ("r_m1", 5), ("hidA", 1), ("hidA", 2), ("r_su", 5), ("hidA", 3),
    ("r_su", 4), ("hidA", 4), ("r_m0", 4), ("hidA", 5), ("g_end", 3),
    ("g_end", 6), ("r_m1", 4), ("r_ao", 0), ("g_end", 4), ("s_x",),
    ("r_ad", 0), ("r_au", 1), ("hidA", 6), ("g_end", 5), ("hidB", 0),
    ("hidB", 1), ("hidB", 2), ("r_m0", 1), ("r_ad", 1), ("r_m1", 1),
    ("r_y", 3), ("hidB", 3), ("r_end", 6), ("r_y", 5), ("hidB", 4),
    ("s_end",), ("r_y", 4), ("r_end", 2), ("r_au", 0), ("r_m0", 0),
    ("r_m1", 0), ("hidB", 5), ("hidB", 6), ("r_end", 5), ("r_end", 3),
    ("r_end", 1), ("r_end", 4), ("r_end", 0),
)

ADAPTER_SCALE = 2.0
LEARN_RATE = 0.001
BETA_ONE = 0.9
BETA_TWO = 0.999
ADAM_EPS = 1e-08


def moment_optimizer_step(param, moment, second, grad):
    new_moment = BETA_ONE * moment + (1.0 - BETA_ONE) * grad
    new_second = BETA_TWO * second + (1.0 - BETA_TWO) * grad * grad
    fix_one = 1.0 - BETA_ONE**STEP
    fix_two = 1.0 - BETA_TWO**STEP
    new_param = param - LEARN_RATE * (new_moment / fix_one) / (
        jnp.sqrt(new_second / fix_two) + ADAM_EPS
    )
    return (new_param, new_moment, new_second)


def nt_dot(a, b):
    return lax.dot_general(a, b, (((1,), (1,)), ((), ())), preferred_element_type=F32)


def tn_dot(a, b):
    return lax.dot_general(a, b, (((0,), (0,)), ((), ())), preferred_element_type=F32)


def nn_dot(a, b):
    return jnp.dot(a, b, preferred_element_type=F32)


G_X, G_U, G_D, G_XU, G_XD, G_O0, G_O1, G_XO0, G_XO1 = range(9)
R_F0, R_F1, R_D0, R_D1, R_U0, R_U1, R_X = range(7)
M_X, M_U, M_D, M_XU, M_XD, M_O, M_XO = range(7)
S_F0, S_F1, S_D0, S_D1, S_U0, S_U1, S_X = range(4, 11)


def kernel(
    grad_scale,
    hid,
    w,
    cot,
    amap,
    bmap,
    lst,
    slots,
    outv,
    hv,
    gtot,
    wv,
    cotf,
    part,
    qf0,
    qf1,
    qru,
    qrd,
    qx,
    pf0,
    pf1,
    pru,
    prd,
    px,
    am32,
    bm32,
    aall,
    acat,
    mask,
    rk,
    rr,
    tot,
    lix,
    lbx,
    gslot,
    con,
    sb,
    gf,
    grd,
    gru,
    gx,
    ld_sem,
    w_sem,
    g_ss,
    g_rs,
    r_ss,
    r_rs,
    k_ss,
    k_rs,
    m_ss,
    m_rs,
    b_ss,
    b_rs,
    s_ss,
    s_rs,
):
    feat = cot.shape[1]
    units = hid.shape[1]
    rows_n = hid.shape[0]
    me = lax.axis_index("tp")
    xl, y = lax.div(me, NY), lax.rem(me, NY)
    ox = 1 - xl
    yu, yd, yo = lax.rem(y + 1, NY), lax.rem(y + 3, NY), lax.rem(y + 2, NY)
    t_x, t_u, t_d, t_o = ox * NY + y, xl * NY + yu, xl * NY + yd, xl * NY + yo
    t_xu, t_xd, t_xo = ox * NY + yu, ox * NY + yd, ox * NY + yo
    g = lax.axis_index("grp")
    xh, z, core = lax.div(g, 2 * NZ), lax.rem(lax.div(g, 2), NZ), lax.rem(g, 2)
    zu, zd, zo = lax.rem(z + 1, NZ), lax.rem(z + 3, NZ), lax.rem(z + 2, NZ)
    oxh = 1 - xh

    def grp_id(a, b, c):
        return a * (2 * NZ) + b * 2 + c

    n_x, n_u, n_d = grp_id(oxh, z, core), grp_id(xh, zu, core), grp_id(xh, zd, core)
    n_s = grp_id(xh, z, 1 - core)

    def col(k):
        return pl.ds(pl.multiple_of(k * feat, 128), feat)

    def seg(s):
        return pl.ds(s * SEG, SEG)

    def half(s, h):
        return pl.ds(s * SEG + h * HALF, HALF)

    ld_a = pltpu.make_async_copy(amap, am32, ld_sem.at[0])
    ld_b = pltpu.make_async_copy(bmap, bm32, ld_sem.at[1])
    ld_h = pltpu.make_async_copy(hid, hv, ld_sem.at[2])
    ld_c = pltpu.make_async_copy(cot, cotf.at[:, col(me)], ld_sem.at[3])
    ld_a.start()
    ld_b.start()
    ld_h.start()
    blocks = [(yq, c) for yq in (yo, yu, yd, y) for c in (0, 1)]
    ld_w = []
    for i, (yq, c) in enumerate(blocks):
        k = c * NY + yq
        ld_w.append(pltpu.make_async_copy(w.at[:, col(k)], wv.at[:, col(k)], w_sem.at[i]))
        ld_w[-1].start()
    ld_c.start()

    barrier = pltpu.get_barrier_semaphore()
    for i in range(1, 2 * NY):
        pl.semaphore_signal(
            barrier, inc=1, device_id={"tp": lax.rem(me + i, 2 * NY)}, device_id_type=MESH
        )
    for dev in (n_x, n_u, n_d, n_s):
        pl.semaphore_signal(barrier, inc=1, device_id={"grp": dev}, device_id_type=MESH)

    ld_a.wait()
    ld_b.wait()
    aall[g, :, pl.ds(0, units)] = am32[...].astype(BF)
    aall[g, :, pl.ds(units, feat)] = bm32[...].astype(BF)

    lane = lax.broadcasted_iota(jnp.int32, (SEG, WIDE), 1)
    unit = lax.shift_right_logical(lane, 6).astype(F32)
    for s in range(SEGS):
        line = jnp.broadcast_to(slots[pl.ds(s, 1), :].astype(F32), (SEG, SEG))
        wide = jnp.concatenate([line.T] * (WIDE // SEG), axis=1)
        mask[seg(s), :] = jnp.where(wide == unit, 1.0, 0.0).astype(BF)

    pl.semaphore_wait(barrier, 2 * NY - 1 + 4)

    sends = []

    def push(src, dst, ss, rs, axis, dev):
        c = pltpu.make_async_remote_copy(
            src_ref=src,
            dst_ref=dst,
            send_sem=ss,
            recv_sem=rs,
            device_id={axis: dev},
            device_id_type=MESH,
        )
        c.start()
        sends.append(c)

    def arrived(dst, ss, rs, axis):
        pltpu.make_async_remote_copy(
            src_ref=dst,
            dst_ref=dst,
            send_sem=ss,
            recv_sem=rs,
            device_id={axis: me if axis == "tp" else g},
            device_id_type=MESH,
        ).wait_recv()

    def g_push(slot, s, rows, k, dev, src=None):
        ref = cotf.at[rows, col(k)]
        push(ref if src is None else src, ref, g_ss.at[slot, s], g_rs.at[slot, s], "tp", dev)

    def g_wait(slot, s, rows, k):
        arrived(cotf.at[rows, col(k)], g_ss.at[slot, s], g_rs.at[slot, s], "tp")

    def gs_x(s):
        g_push(G_X, s, seg(s), me, t_x, cot.at[seg(s), :])

    def gs_u(s):
        g_push(G_D, s, seg(s), me, t_u, cot.at[seg(s), :])

    def gs_d(s):
        g_push(G_U, s, seg(s), me, t_d, cot.at[seg(s), :])

    def g_x(s):
        g_wait(G_X, s, seg(s), t_x)
        g_push(G_XD, s, seg(s), t_x, t_u)
        g_push(G_XU, s, seg(s), t_x, t_d)

    def g_d(s):
        g_wait(G_D, s, seg(s), t_d)
        g_push(G_O0, s, half(s, 0), t_d, t_u)
        if s in Y_FIRST:
            g_push(G_XD, s, seg(s), t_d, t_x)

    def g_u(s):
        g_wait(G_U, s, seg(s), t_u)
        g_push(G_O1, s, half(s, 1), t_u, t_d)
        if s in Y_FIRST:
            g_push(G_XU, s, seg(s), t_u, t_x)

    def g_xd(s):
        g_wait(G_XD, s, seg(s), t_xd)
        g_push(G_XO0, s, half(s, 0), t_xd, t_u)

    def g_xu(s):
        g_wait(G_XU, s, seg(s), t_xu)
        g_push(G_XO1, s, half(s, 1), t_xu, t_d)

    def g_o0(s):
        g_wait(G_O0, s, half(s, 0), t_o)
        g_push(G_XO0, s, half(s, 0), t_o, t_x)

    def g_o1(s):
        g_wait(G_O1, s, half(s, 1), t_o)
        g_push(G_XO1, s, half(s, 1), t_o, t_x)

    def g_end(s):
        if s in Y_FIRST:
            g_wait(G_X, s, seg(s), t_x)
            g_wait(G_XD, s, seg(s), t_xd)
            g_wait(G_XU, s, seg(s), t_xu)
        else:
            g_wait(G_O0, s, half(s, 0), t_o)
            g_wait(G_O1, s, half(s, 1), t_o)
        g_wait(G_XO0, s, half(s, 0), t_xo)
        g_wait(G_XO1, s, half(s, 1), t_xo)

    def m_push(slot, o, dev):
        push(aall.at[o], aall.at[o], m_ss.at[slot], m_rs.at[slot], "grp", dev)

    def m_wait(slot, o):
        arrived(aall.at[o], m_ss.at[slot], m_rs.at[slot], "grp")

    def b_push(i, o):
        push(aall.at[o], aall.at[o], b_ss.at[i], b_rs.at[i], "grp", n_s)

    def m_start():
        m_push(M_X, g, n_x)
        m_push(M_D, g, n_u)
        m_push(M_U, g, n_d)
        b_push(7, g)

    def m_x():
        m_wait(M_X, n_x)
        m_push(M_XD, n_x, n_u)
        m_push(M_XU, n_x, n_d)
        b_push(M_X, n_x)

    def m_d():
        m_wait(M_D, n_d)
        m_push(M_O, n_d, n_u)
        b_push(M_D, n_d)

    def m_u():
        m_wait(M_U, n_u)
        b_push(M_U, n_u)

    def m_xu():
        m_wait(M_XU, grp_id(oxh, zu, core))
        m_push(M_XO, grp_id(oxh, zu, core), n_d)
        b_push(M_XU, grp_id(oxh, zu, core))

    def m_xd():
        m_wait(M_XD, grp_id(oxh, zd, core))
        b_push(M_XD, grp_id(oxh, zd, core))

    def m_o():
        m_wait(M_O, grp_id(xh, zo, core))
        b_push(M_O, grp_id(xh, zo, core))

    def m_xo():
        m_wait(M_XO, grp_id(oxh, zo, core))
        b_push(M_XO, grp_id(oxh, zo, core))

    def m_end():
        sib = 1 - core
        for i, o in (
            (7, grp_id(xh, z, sib)),
            (M_X, grp_id(oxh, z, sib)),
            (M_D, grp_id(xh, zd, sib)),
            (M_U, grp_id(xh, zu, sib)),
            (M_XU, grp_id(oxh, zu, sib)),
            (M_XD, grp_id(oxh, zd, sib)),
            (M_O, grp_id(xh, zo, sib)),
            (M_XO, grp_id(oxh, zo, sib)),
        ):
            arrived(aall.at[o], b_ss.at[i], b_rs.at[i], "grp")

    def part_block(i):
        if i == 0:
            ld_h.wait()
        yq, c = blocks[i]
        k = c * NY + yq
        ld_w[i].wait()
        step = feat // 2

        @pl.loop(0, 2)
        def _(j):
            wt = wv[:, pl.ds(pl.multiple_of(k * feat + j * step, 128), step)]
            at = pl.ds(pl.multiple_of(c * feat + j * step, 128), step)
            part[yq, :, at] = nn_dot(hv[...], wt).astype(BF)

    def r_push(src, dst, slot, s, dev):
        push(src, dst, r_ss.at[slot, s], r_rs.at[slot, s], "tp", dev)

    def r_wait(dst, slot, s):
        arrived(dst, r_ss.at[slot, s], r_rs.at[slot, s], "tp")

    def bufs(s):
        if s in Y_SUMS:
            i = Y_SUMS.index(s)
            return qf0.at[i], qf1.at[i], qru.at[i], qrd.at[i], pl.ds(0, 2 * feat)
        i = X_SUMS.index(s)
        return pf0.at[i], pf1.at[i], pru.at[i], prd.at[i], col(xl)

    h0, h1 = pl.ds(0, HALF), pl.ds(HALF, HALF)

    def add_into(ref, idx, other):
        ref[idx] = (ref[idx].astype(F32) + other.astype(F32)).astype(BF)

    def r_so(s):
        f0, f1, _, _, cs = bufs(s)
        r_push(part.at[yo, half(s, 0), cs], f0, R_F0, s, t_u)
        r_push(part.at[yo, half(s, 1), cs], f1, R_F1, s, t_d)

    def r_su(s):
        _, _, _, rd, cs = bufs(s)
        r_push(part.at[yu, half(s, 1), cs], rd.at[h1, :], R_D1, s, t_u)

    def r_sd(s):
        _, _, ru, _, cs = bufs(s)
        r_push(part.at[yd, half(s, 0), cs], ru.at[h0, :], R_U0, s, t_d)

    def r_x(j, yq):
        def send(s):
            i = X_SUMS.index(s)
            r_push(part.at[yq, seg(s), col(ox)], px.at[i, j], R_X + j, s, t_x)

        return send

    def r_add(j, yq, after):
        def add(s):
            i = X_SUMS.index(s)
            r_wait(px.at[i, j], R_X + j, s)
            add_into(part, (yq, seg(s), col(xl)), px[i, j])
            after(s)

        return add

    def r_m0(s):
        f0, _, _, rd, cs = bufs(s)
        r_wait(f0, R_F0, s)
        add_into(part, (yu, half(s, 0), cs), f0[...])
        r_push(part.at[yu, half(s, 0), cs], rd.at[h0, :], R_D0, s, t_u)

    def r_m1(s):
        _, f1, ru, _, cs = bufs(s)
        r_wait(f1, R_F1, s)
        add_into(part, (yd, half(s, 1), cs), f1[...])
        r_push(part.at[yd, half(s, 1), cs], ru.at[h1, :], R_U1, s, t_d)

    def y_wait(s):
        _, _, ru, rd, _ = bufs(s)
        r_wait(rd.at[h0, :], R_D0, s)
        r_wait(rd.at[h1, :], R_D1, s)
        r_wait(ru.at[h0, :], R_U0, s)
        r_wait(ru.at[h1, :], R_U1, s)

    def y_total(s, cs):
        i = Y_SUMS.index(s)
        return (
            part[y, seg(s), cs].astype(F32)
            + qru[i, :, cs].astype(F32)
            + qrd[i, :, cs].astype(F32)
        )

    def r_y(s):
        y_wait(s)
        part[y, seg(s), col(ox)] = y_total(s, col(ox)).astype(BF)
        r_push(part.at[y, seg(s), col(ox)], qx.at[Y_SUMS.index(s)], R_X, s, t_x)

    def r_end(s):
        if s in Y_SUMS:
            i = Y_SUMS.index(s)
            r_wait(qx.at[i], R_X, s)
            total = y_total(s, col(xl)) + qx[i].astype(F32)
        else:
            i = X_SUMS.index(s)
            r_wait(px.at[i, 3], R_X + 3, s)
            y_wait(s)
            total = (
                part[y, seg(s), col(xl)].astype(F32)
                + px[i, 3].astype(F32)
                + pru[i].astype(F32)
                + prd[i].astype(F32)
            )
        lora = nn_dot(lix[seg(s), :], acat[:, pl.ds(units, feat)])
        outv[seg(s), :] = (total + ADAPTER_SCALE * lora).astype(BF)

    def pick(shape, dim, shift):
        i = jnp.bitwise_and(lax.broadcasted_iota(jnp.int32, shape, dim), RANK - 1)
        j = lax.broadcasted_iota(jnp.int32, shape, 1 - dim)
        return jnp.where(i + shift == j, 1.0, 0.0).astype(BF)

    def rank_start():
        ld_c.wait()
        for u in range(USE):
            acat[pl.ds(u * RANK, RANK), :] = aall[lst[0, u]]
        m = mask[...].astype(F32)
        down = (nt_dot(hv[...], acat[:, pl.ds(0, units)]) * m).astype(BF)
        back = (nt_dot(cotf[:, col(me)], acat[:, pl.ds(units, feat)]) * m).astype(BF)
        rk[...] = (
            nn_dot(down, pick((WIDE, 2 * RANK), 0, 0))
            + nn_dot(back, pick((WIDE, 2 * RANK), 0, RANK))
        ).astype(BF)
        n = rows_n // (2 * NY)
        for i in range(1, 2 * NY):
            dev = lax.rem(me + i, 2 * NY)
            src = rk.at[pl.ds(pl.multiple_of(dev * n, 16), n), :]
            push(src, rr.at[i], k_ss.at[0, i], k_rs.at[0, i], "tp", dev)

    def rank_sum():
        n = rows_n // (2 * NY)
        mine = pl.ds(pl.multiple_of(me * n, 16), n)
        total = rk[mine, :].astype(F32)
        for i in range(1, 2 * NY):
            arrived(rr.at[i], k_ss.at[0, i], k_rs.at[0, i], "tp")
            total = total + rr[i].astype(F32)
        tot[mine, :] = total.astype(BF)
        for i in range(1, 2 * NY):
            dev = lax.rem(me + i, 2 * NY)
            push(tot.at[mine, :], tot.at[mine, :], k_ss.at[1, i], k_rs.at[1, i], "tp", dev)

    def rank_end():
        n = rows_n // (2 * NY)
        for i in range(1, 2 * NY):
            src = lax.rem(me + 2 * NY - i, 2 * NY)
            theirs = pl.ds(pl.multiple_of(src * n, 16), n)
            arrived(tot.at[theirs, :], k_ss.at[1, i], k_rs.at[1, i], "tp")
        m = mask[...].astype(F32)
        lix[...] = (nn_dot(tot[...], pick((2 * RANK, WIDE), 1, 0)) * m).astype(BF)
        lbx[...] = (nn_dot(tot[...], pick((2 * RANK, WIDE), 1, RANK)) * m).astype(BF)

    def grads():
        step = 256
        wide = units + feat

        @pl.loop(0, units // step)
        def _(j):
            at = pl.ds(pl.multiple_of(j * step, 128), step)
            ga = tn_dot(lbx[...], hv[:, at]) * grad_scale
            for u in range(USE):
                gslot[u, :, at] = ga[u * RANK : (u + 1) * RANK, :].astype(BF)

        gb = tn_dot(lix[...], cotf[:, col(me)]) * grad_scale
        for u in range(USE):
            gslot[u, :, pl.ds(units, feat)] = gb[u * RANK : (u + 1) * RANK, :].astype(BF)
        gslot[USE] = jnp.zeros((RANK, wide), BF)
        for o in range(4 * NZ):
            at = jnp.int32(USE)
            for u in range(USE):
                at = jnp.where(lst[0, u] == o, u, at)
            con[o % 2, (o // 2) % NZ, o // (2 * NZ)] = gslot[at]

    def s_push(src, dst, slot, dev):
        push(src, dst, s_ss.at[slot], s_rs.at[slot], "grp", dev)

    def s_wait(dst, slot):
        arrived(dst, s_ss.at[slot], s_rs.at[slot], "grp")

    def sum_start():
        for i, zq in enumerate((zo, zu, zd, z)):
            s_push(con.at[1 - core, zq], sb.at[zq], i, n_s)

    def s_o():
        s_wait(sb.at[zo], 0)
        add_into(con, (core, zo), sb[zo])
        s_push(con.at[core, zo, 0], gf.at[0], S_F0, n_u)
        s_push(con.at[core, zo, 1], gf.at[1], S_F1, n_d)

    def s_u():
        s_wait(sb.at[zu], 1)
        add_into(con, (core, zu), sb[zu])
        s_push(con.at[core, zu, 1], grd.at[1], S_D1, n_u)

    def s_d():
        s_wait(sb.at[zd], 2)
        add_into(con, (core, zd), sb[zd])
        s_push(con.at[core, zd, 0], gru.at[0], S_U0, n_d)

    def s_m0():
        s_wait(gf.at[0], S_F0)
        add_into(con, (core, zu, 0), gf[0])
        s_push(con.at[core, zu, 0], grd.at[0], S_D0, n_u)

    def s_m1():
        s_wait(gf.at[1], S_F1)
        add_into(con, (core, zd, 1), gf[1])
        s_push(con.at[core, zd, 1], gru.at[1], S_U1, n_d)

    def sum_total(h):
        return (
            con[core, z, h].astype(F32)
            + sb[z, h].astype(F32)
            + grd[h].astype(F32)
            + gru[h].astype(F32)
        )

    def s_x():
        s_wait(sb.at[z], 3)
        s_wait(grd.at[1], S_D1)
        s_wait(gru.at[0], S_U0)
        s_wait(grd.at[0], S_D0)
        s_wait(gru.at[1], S_U1)
        con[core, z, oxh] = sum_total(oxh).astype(BF)
        s_push(con.at[core, z, oxh], gx, S_X, n_x)

    def s_end():
        s_wait(gx, S_X)
        gtot[...] = sum_total(xh) + gx[...].astype(F32)

    def hidden_tile(part_no):
        rows = pl.ds(0, CUT) if part_no == 0 else pl.ds(CUT, rows_n - CUT)

        def tile(j):
            at = pl.ds(j * 256, 256)
            r = nt_dot(cotf[rows, :], wv[at, :])
            r = r + ADAPTER_SCALE * nn_dot(lbx[rows, :], acat[:, at])
            hv[rows, at] = r.astype(BF)

        return tile

    tasks = dict(
        gs_x=gs_x,
        gs_u=gs_u,
        gs_d=gs_d,
        g_x=g_x,
        g_d=g_d,
        g_u=g_u,
        g_xd=g_xd,
        g_xu=g_xu,
        g_o0=g_o0,
        g_o1=g_o1,
        g_end=g_end,
        m_start=m_start,
        m_x=m_x,
        m_d=m_d,
        m_u=m_u,
        m_xu=m_xu,
        m_xd=m_xd,
        m_o=m_o,
        m_xo=m_xo,
        m_end=m_end,
        part=part_block,
        r_so=r_so,
        r_su=r_su,
        r_sd=r_sd,
        r_xo=r_x(0, yo),
        r_xu=r_x(1, yu),
        r_xd=r_x(2, yd),
        r_xm=r_x(3, y),
        r_ao=r_add(0, yo, r_so),
        r_au=r_add(1, yu, r_su),
        r_ad=r_add(2, yd, r_sd),
        r_m0=r_m0,
        r_m1=r_m1,
        r_y=r_y,
        r_end=r_end,
        rank_start=rank_start,
        rank_sum=rank_sum,
        rank_end=rank_end,
        grads=grads,
        sum_start=sum_start,
        s_o=s_o,
        s_u=s_u,
        s_d=s_d,
        s_m0=s_m0,
        s_m1=s_m1,
        s_x=s_x,
        s_end=s_end,
        hidA=hidden_tile(0),
        hidB=hidden_tile(1),
    )
    for name, *index in ORDER:
        tasks[name](*index)
    for c in sends:
        c.wait_send()


def fused(hidden, w, cot, amap, bmap, lst, slots, rows_all):
    rows, units = hidden.shape
    feat = cot.shape[1]
    wide = units + feat
    nq, np_ = len(Y_SUMS), len(X_SUMS)
    any_ = pl.BlockSpec(memory_space=pl.ANY)
    dma = pltpu.SemaphoreType.DMA
    v = pltpu.VMEM
    return pl.pallas_call(
        functools.partial(kernel, ADAPTER_SCALE / rows_all),
        out_shape=(
            pltpu.VMEM((rows, feat), BF),
            pltpu.VMEM((rows, units), BF),
            pltpu.VMEM((RANK, wide), F32),
        ),
        in_specs=[any_] * 5
        + [pl.BlockSpec(memory_space=pltpu.SMEM), pl.BlockSpec(memory_space=pltpu.VMEM)],
        out_specs=(pl.BlockSpec(memory_space=pltpu.VMEM),) * 3,
        scratch_shapes=[
            v((units, 2 * NY * feat), BF),
            v((rows, 2 * NY * feat), BF),
            v((NY, rows, 2 * feat), BF),
            v((nq, HALF, 2 * feat), BF),
            v((nq, HALF, 2 * feat), BF),
            v((nq, SEG, 2 * feat), BF),
            v((nq, SEG, 2 * feat), BF),
            v((nq, SEG, feat), BF),
            v((np_, HALF, feat), BF),
            v((np_, HALF, feat), BF),
            v((np_, SEG, feat), BF),
            v((np_, SEG, feat), BF),
            v((np_, NY, SEG, feat), BF),
            v((RANK, units), F32),
            v((RANK, feat), F32),
            v((4 * NZ, RANK, wide), BF),
            v((WIDE, wide), BF),
            v((rows, WIDE), BF),
            v((rows, 2 * RANK), BF),
            v((2 * NY, rows // (2 * NY), 2 * RANK), BF),
            v((rows, 2 * RANK), BF),
            v((rows, WIDE), BF),
            v((rows, WIDE), BF),
            v((USE + 1, RANK, wide), BF),
            v((2, NZ, 2, RANK, wide), BF),
            v((NZ, 2, RANK, wide), BF),
            v((2, RANK, wide), BF),
            v((2, RANK, wide), BF),
            v((2, RANK, wide), BF),
            v((RANK, wide), BF),
            dma((4,)),
            dma((2 * NY,)),
            dma((9, SEGS)),
            dma((9, SEGS)),
            dma((10, SEGS)),
            dma((10, SEGS)),
            dma((2, 2 * NY)),
            dma((2, 2 * NY)),
            dma((7,)),
            dma((7,)),
            dma((8,)),
            dma((8,)),
            dma((11,)),
            dma((11,)),
        ],
        compiler_params=pltpu.CompilerParams(
            collective_id=0,
            has_side_effects=True,
            vmem_limit_bytes=56 * 1024 * 1024,
        ),
    )(hidden, w, cot, amap, bmap, lst, slots)


def per_device(
    hidden,
    frozen_down_matrix,
    cotangent,
    adapter_input_maps,
    adapter_output_maps,
    input_first_moment,
    input_second_moment,
    output_first_moment,
    output_second_moment,
    group_adapter_list,
    token_adapter_slot,
):
    rows_all = hidden.shape[0] * lax.axis_size("grp")
    output, hidden_gradient, grad = fused(
        hidden,
        frozen_down_matrix,
        cotangent,
        adapter_input_maps[0],
        adapter_output_maps[0],
        group_adapter_list,
        token_adapter_slot.reshape(SEGS, SEG),
        rows_all,
    )
    units = hidden.shape[1]
    new_a, new_a_m, new_a_v = moment_optimizer_step(
        adapter_input_maps, input_first_moment, input_second_moment, grad[None, :, :units]
    )
    new_b, new_b_m, new_b_v = moment_optimizer_step(
        adapter_output_maps, output_first_moment, output_second_moment, grad[None, :, units:]
    )
    return (output, hidden_gradient, new_a, new_b, new_a_m, new_a_v, new_b_m, new_b_v)


def solution(mesh):
    return jax.shard_map(
        per_device,
        mesh=mesh,
        in_specs=(
            P("grp", "tp"),
            P("tp", None),
            P("grp", "tp"),
            P("grp", None, "tp"),
            P("grp", None, "tp"),
            P("grp", None, "tp"),
            P("grp", None, "tp"),
            P("grp", None, "tp"),
            P("grp", None, "tp"),
            P("grp", None),
            P("grp"),
        ),
        out_specs=(
            P("grp", "tp"),
            P("grp", "tp"),
            P("grp", None, "tp"),
            P("grp", None, "tp"),
            P("grp", None, "tp"),
            P("grp", None, "tp"),
            P("grp", None, "tp"),
            P("grp", None, "tp"),
        ),
        check_vma=False,
    )
```

```python
import functools

import jax
import jax.numpy as jnp
from jax import lax
from jax.experimental import pallas as pl
from jax.experimental.pallas import tpu as pltpu
from jax.sharding import PartitionSpec as P

MESH = pl.DeviceIdType.MESH
BF = jnp.bfloat16
F32 = jnp.float32

SEG = 128
HALF = 64
SEGS = 7
USE = 4
STEP = 20
RANK = 64
WIDE = USE * RANK
NY = 4
NZ = 4
Y_FIRST = (5, 6)
X_SUMS = (0, 1, 2)
Y_SUMS = tuple(s for s in range(SEGS) if s not in X_SUMS)
CUT = 3 * SEG

ORDER = (
    ("gs_x", 0), ("gs_u", 3), ("gs_d", 1), ("m_start",), ("gs_d", 4),
    ("gs_d", 2), ("gs_u", 5), ("gs_x", 3), ("part", 0), ("part", 1),
    ("r_so", 6), ("r_xo", 2), ("r_xo", 1), ("r_so", 3), ("part", 2),
    ("gs_u", 1), ("part", 3), ("r_su", 6), ("r_su", 3), ("g_d", 5),
    ("r_xu", 2), ("m_d",), ("gs_d", 0), ("gs_x", 4), ("m_x",),
    ("m_u",), ("part", 4), ("gs_d", 5), ("r_so", 5), ("part", 5),
    ("r_xd", 2), ("r_su", 5), ("g_u", 4), ("part", 6), ("r_xd", 0),
    ("g_x", 0), ("sent", 13), ("m_xu",), ("r_sd", 6), ("gs_u", 2),
    ("gs_x", 2), ("g_u", 0), ("part", 7), ("m_xd",), ("r_xm", 0),
    ("g_d", 1), ("mask",), ("g_u", 1), ("g_u", 2), ("gs_u", 0),
    ("m_o",), ("r_m1", 5), ("sent", 22), ("m_xo",), ("gs_u", 6),
    ("sent", 26), ("m_end",), ("rank_start",), ("gs_d", 3), ("gs_x", 1),
    ("g_o0", 5), ("sent", 37), ("g_x", 2), ("sent", 43), ("rank_x",),
    ("r_xm", 2), ("g_x", 3), ("sent", 55), ("g_x", 1), ("gs_x", 5),
    ("rank_sum",), ("g_xu", 2), ("g_u", 5), ("r_xu", 1), ("r_ao", 1),
    ("g_x", 4), ("g_xd", 2), ("rank_y",), ("g_xu", 0), ("g_xd", 1),
    ("g_u", 3), ("r_ao", 2), ("gs_d", 6), ("sent", 68), ("g_o1", 5),
    ("g_xd", 0), ("g_xu", 3), ("gs_x", 6), ("g_d", 6), ("g_d", 2),
    ("g_xd", 3), ("g_d", 0), ("gs_u", 4), ("r_xd", 1), ("r_xo", 0),
    ("r_sd", 5), ("r_xm", 1), ("g_xu", 1), ("r_so", 4), ("r_m0", 5),
    ("sent", 75), ("rank_end",), ("grads",), ("sum_start",), ("sent", 88),
    ("s_o",), ("g_end", 0), ("g_u", 6), ("r_m1", 3), ("g_xu", 4),
    ("r_sd", 3), ("s_u",), ("g_xd", 4), ("r_m0", 3), ("g_end", 2),
    ("r_m1", 6), ("sent", 92), ("g_d", 4), ("r_ad", 1), ("r_m1", 1),
    ("g_o0", 6), ("g_d", 3), ("r_xu", 0), ("sent", 99), ("g_end", 1),
    ("r_m0", 6), ("r_ao", 0), ("s_d",), ("r_su", 4), ("hidA", 0),
    ("hidA", 1), ("hidA", 2), ("hidA", 3), ("r_y", 5), ("g_o1", 6),
    ("r_au", 2), ("r_m0", 2), ("r_m1", 4), ("r_sd", 4), ("r_ad", 2),
    ("s_m0",), ("r_m0", 4), ("r_m1", 2), ("s_m1",), ("hidA", 4),
    ("sent", 115), ("r_au", 0), ("r_y", 3), ("hidA", 5), ("g_end", 4),
    ("hidA", 6), ("r_au", 1), ("r_m0", 1), ("r_y", 6), ("r_end", 5),
    ("g_end", 5), ("g_end", 3), ("g_end", 6), ("hidB", 0), ("hidB", 1),
    ("s_x",), ("hidB", 2), ("hidB", 3), ("r_ad", 0), ("r_m1", 0),
    ("r_m0", 0), ("hidB", 4), ("r_end", 6), ("sent", 137), ("r_y", 4),
    ("r_end", 3), ("hidB", 5), ("hidB", 6), ("r_end", 2), ("r_end", 1),
    ("s_end",), ("sent", 143), ("r_end", 0), ("r_end", 4),
)

ADAPTER_SCALE = 2.0
LEARN_RATE = 0.001
BETA_ONE = 0.9
BETA_TWO = 0.999
ADAM_EPS = 1e-08


def moment_optimizer_step(param, moment, second, grad):
    new_moment = BETA_ONE * moment + (1.0 - BETA_ONE) * grad
    new_second = BETA_TWO * second + (1.0 - BETA_TWO) * grad * grad
    fix_one = 1.0 - BETA_ONE**STEP
    fix_two = 1.0 - BETA_TWO**STEP
    new_param = param - LEARN_RATE * (new_moment / fix_one) / (
        jnp.sqrt(new_second / fix_two) + ADAM_EPS
    )
    return (new_param, new_moment, new_second)


def nt_dot(a, b):
    return lax.dot_general(a, b, (((1,), (1,)), ((), ())), preferred_element_type=F32)


def tn_dot(a, b):
    return lax.dot_general(a, b, (((0,), (0,)), ((), ())), preferred_element_type=F32)


def nn_dot(a, b):
    return jnp.dot(a, b, preferred_element_type=F32)


G_X, G_U, G_D, G_XU, G_XD, G_O0, G_O1, G_XO0, G_XO1 = range(9)
R_F0, R_F1, R_D0, R_D1, R_U0, R_U1, R_X = range(7)
M_X, M_U, M_D, M_XU, M_XD, M_O, M_XO = range(7)
S_F0, S_F1, S_D0, S_D1, S_U0, S_U1, S_X = range(4, 11)


def kernel(
    grad_scale,
    hid,
    w,
    cot,
    amap,
    bmap,
    lst,
    slots,
    outv,
    hv,
    gtot,
    wv,
    cotf,
    part,
    qf0,
    qf1,
    qru,
    qrd,
    qx,
    pf0,
    pf1,
    pru,
    prd,
    px,
    am32,
    bm32,
    aall,
    acat,
    mask,
    rk,
    kx,
    rr,
    tot,
    lix,
    lbx,
    gslot,
    con,
    sb,
    gf,
    grd,
    gru,
    gx,
    ld_sem,
    w_sem,
    g_ss,
    g_rs,
    r_ss,
    r_rs,
    k_ss,
    k_rs,
    m_ss,
    m_rs,
    b_ss,
    b_rs,
    s_ss,
    s_rs,
):
    feat = cot.shape[1]
    units = hid.shape[1]
    rows_n = hid.shape[0]
    me = lax.axis_index("tp")
    xl, y = lax.div(me, NY), lax.rem(me, NY)
    ox = 1 - xl
    yu, yd, yo = lax.rem(y + 1, NY), lax.rem(y + 3, NY), lax.rem(y + 2, NY)
    t_x, t_u, t_d, t_o = ox * NY + y, xl * NY + yu, xl * NY + yd, xl * NY + yo
    t_xu, t_xd, t_xo = ox * NY + yu, ox * NY + yd, ox * NY + yo
    g = lax.axis_index("grp")
    xh, z, core = lax.div(g, 2 * NZ), lax.rem(lax.div(g, 2), NZ), lax.rem(g, 2)
    zu, zd, zo = lax.rem(z + 1, NZ), lax.rem(z + 3, NZ), lax.rem(z + 2, NZ)
    oxh = 1 - xh

    def grp_id(a, b, c):
        return a * (2 * NZ) + b * 2 + c

    n_x, n_u, n_d = grp_id(oxh, z, core), grp_id(xh, zu, core), grp_id(xh, zd, core)
    n_s = grp_id(xh, z, 1 - core)

    def col(k):
        return pl.ds(pl.multiple_of(k * feat, 128), feat)

    def seg(s):
        return pl.ds(s * SEG, SEG)

    def half(s, h):
        return pl.ds(s * SEG + h * HALF, HALF)

    barrier = pltpu.get_barrier_semaphore()
    for dev in (t_x, t_u, t_d, t_o):
        pl.semaphore_signal(barrier, inc=1, device_id={"tp": dev}, device_id_type=MESH)
    for dev in (n_x, n_u, n_d, n_s):
        pl.semaphore_signal(barrier, inc=1, device_id={"grp": dev}, device_id_type=MESH)

    ld_a = pltpu.make_async_copy(amap, am32, ld_sem.at[0])
    ld_b = pltpu.make_async_copy(bmap, bm32, ld_sem.at[1])
    ld_h = pltpu.make_async_copy(hid, hv, ld_sem.at[2])
    ld_c = pltpu.make_async_copy(cot, cotf.at[:, col(me)], ld_sem.at[3])
    ld_a.start()
    ld_b.start()
    ld_h.start()
    blocks = [(yq, c) for yq in (yo, yu, yd, y) for c in (0, 1)]
    ld_w = []
    for i, (yq, c) in enumerate(blocks):
        k = c * NY + yq
        ld_w.append(pltpu.make_async_copy(w.at[:, col(k)], wv.at[:, col(k)], w_sem.at[i]))
        ld_w[-1].start()
    ld_c.start()

    pl.semaphore_wait(barrier, 8)

    sends = []

    def push(src, dst, ss, rs, axis, dev):
        c = pltpu.make_async_remote_copy(
            src_ref=src,
            dst_ref=dst,
            send_sem=ss,
            recv_sem=rs,
            device_id={axis: dev},
            device_id_type=MESH,
        )
        c.start()
        sends.append(c)

    def arrived(dst, ss, rs, axis):
        pltpu.make_async_remote_copy(
            src_ref=dst,
            dst_ref=dst,
            send_sem=ss,
            recv_sem=rs,
            device_id={axis: me if axis == "tp" else g},
            device_id_type=MESH,
        ).wait_recv()

    def g_push(slot, s, rows, k, dev, src=None):
        ref = cotf.at[rows, col(k)]
        push(ref if src is None else src, ref, g_ss.at[slot, s], g_rs.at[slot, s], "tp", dev)

    def g_wait(slot, s, rows, k):
        arrived(cotf.at[rows, col(k)], g_ss.at[slot, s], g_rs.at[slot, s], "tp")

    def gs_x(s):
        g_push(G_X, s, seg(s), me, t_x, cot.at[seg(s), :])

    def gs_u(s):
        g_push(G_D, s, seg(s), me, t_u, cot.at[seg(s), :])

    def gs_d(s):
        g_push(G_U, s, seg(s), me, t_d, cot.at[seg(s), :])

    def g_x(s):
        g_wait(G_X, s, seg(s), t_x)
        g_push(G_XD, s, seg(s), t_x, t_u)
        g_push(G_XU, s, seg(s), t_x, t_d)

    def g_d(s):
        g_wait(G_D, s, seg(s), t_d)
        g_push(G_O0, s, half(s, 0), t_d, t_u)
        if s in Y_FIRST:
            g_push(G_XD, s, seg(s), t_d, t_x)

    def g_u(s):
        g_wait(G_U, s, seg(s), t_u)
        g_push(G_O1, s, half(s, 1), t_u, t_d)
        if s in Y_FIRST:
            g_push(G_XU, s, seg(s), t_u, t_x)

    def g_xd(s):
        g_wait(G_XD, s, seg(s), t_xd)
        g_push(G_XO0, s, half(s, 0), t_xd, t_u)

    def g_xu(s):
        g_wait(G_XU, s, seg(s), t_xu)
        g_push(G_XO1, s, half(s, 1), t_xu, t_d)

    def g_o0(s):
        g_wait(G_O0, s, half(s, 0), t_o)
        g_push(G_XO0, s, half(s, 0), t_o, t_x)

    def g_o1(s):
        g_wait(G_O1, s, half(s, 1), t_o)
        g_push(G_XO1, s, half(s, 1), t_o, t_x)

    def g_end(s):
        if s in Y_FIRST:
            g_wait(G_X, s, seg(s), t_x)
            g_wait(G_XD, s, seg(s), t_xd)
            g_wait(G_XU, s, seg(s), t_xu)
        else:
            g_wait(G_O0, s, half(s, 0), t_o)
            g_wait(G_O1, s, half(s, 1), t_o)
        g_wait(G_XO0, s, half(s, 0), t_xo)
        g_wait(G_XO1, s, half(s, 1), t_xo)

    def m_push(slot, o, dev):
        push(aall.at[o], aall.at[o], m_ss.at[slot], m_rs.at[slot], "grp", dev)

    def m_wait(slot, o):
        arrived(aall.at[o], m_ss.at[slot], m_rs.at[slot], "grp")

    def b_push(i, o):
        push(aall.at[o], aall.at[o], b_ss.at[i], b_rs.at[i], "grp", n_s)

    def m_start():
        ld_a.wait()
        ld_b.wait()
        aall[g, :, pl.ds(0, units)] = am32[...].astype(BF)
        aall[g, :, pl.ds(units, feat)] = bm32[...].astype(BF)
        m_push(M_X, g, n_x)
        m_push(M_D, g, n_u)
        m_push(M_U, g, n_d)
        b_push(7, g)

    def m_x():
        m_wait(M_X, n_x)
        m_push(M_XD, n_x, n_u)
        m_push(M_XU, n_x, n_d)
        b_push(M_X, n_x)

    def m_d():
        m_wait(M_D, n_d)
        m_push(M_O, n_d, n_u)
        b_push(M_D, n_d)

    def m_u():
        m_wait(M_U, n_u)
        b_push(M_U, n_u)

    def m_xu():
        m_wait(M_XU, grp_id(oxh, zu, core))
        m_push(M_XO, grp_id(oxh, zu, core), n_d)
        b_push(M_XU, grp_id(oxh, zu, core))

    def m_xd():
        m_wait(M_XD, grp_id(oxh, zd, core))
        b_push(M_XD, grp_id(oxh, zd, core))

    def m_o():
        m_wait(M_O, grp_id(xh, zo, core))
        b_push(M_O, grp_id(xh, zo, core))

    def m_xo():
        m_wait(M_XO, grp_id(oxh, zo, core))
        b_push(M_XO, grp_id(oxh, zo, core))

    def m_end():
        sib = 1 - core
        for i, o in (
            (7, grp_id(xh, z, sib)),
            (M_X, grp_id(oxh, z, sib)),
            (M_D, grp_id(xh, zd, sib)),
            (M_U, grp_id(xh, zu, sib)),
            (M_XU, grp_id(oxh, zu, sib)),
            (M_XD, grp_id(oxh, zd, sib)),
            (M_O, grp_id(xh, zo, sib)),
            (M_XO, grp_id(oxh, zo, sib)),
        ):
            arrived(aall.at[o], b_ss.at[i], b_rs.at[i], "grp")

    def part_block(i):
        if i == 0:
            ld_h.wait()
        yq, c = blocks[i]
        k = c * NY + yq
        ld_w[i].wait()
        step = feat // 2

        @pl.loop(0, 2)
        def _(j):
            wt = wv[:, pl.ds(pl.multiple_of(k * feat + j * step, 128), step)]
            at = pl.ds(pl.multiple_of(c * feat + j * step, 128), step)
            part[yq, :, at] = nn_dot(hv[...], wt).astype(BF)

    def r_push(src, dst, slot, s, dev):
        push(src, dst, r_ss.at[slot, s], r_rs.at[slot, s], "tp", dev)

    def r_wait(dst, slot, s):
        arrived(dst, r_ss.at[slot, s], r_rs.at[slot, s], "tp")

    def bufs(s):
        if s in Y_SUMS:
            i = Y_SUMS.index(s)
            return qf0.at[i], qf1.at[i], qru.at[i], qrd.at[i], pl.ds(0, 2 * feat)
        i = X_SUMS.index(s)
        return pf0.at[i], pf1.at[i], pru.at[i], prd.at[i], col(xl)

    h0, h1 = pl.ds(0, HALF), pl.ds(HALF, HALF)

    def add_into(ref, idx, other):
        ref[idx] = (ref[idx].astype(F32) + other.astype(F32)).astype(BF)

    def r_so(s):
        f0, f1, _, _, cs = bufs(s)
        r_push(part.at[yo, half(s, 0), cs], f0, R_F0, s, t_u)
        r_push(part.at[yo, half(s, 1), cs], f1, R_F1, s, t_d)

    def r_su(s):
        _, _, _, rd, cs = bufs(s)
        r_push(part.at[yu, half(s, 1), cs], rd.at[h1, :], R_D1, s, t_u)

    def r_sd(s):
        _, _, ru, _, cs = bufs(s)
        r_push(part.at[yd, half(s, 0), cs], ru.at[h0, :], R_U0, s, t_d)

    def r_x(j, yq):
        def send(s):
            i = X_SUMS.index(s)
            r_push(part.at[yq, seg(s), col(ox)], px.at[i, j], R_X + j, s, t_x)

        return send

    def r_add(j, yq, after):
        def add(s):
            i = X_SUMS.index(s)
            r_wait(px.at[i, j], R_X + j, s)
            add_into(part, (yq, seg(s), col(xl)), px[i, j])
            after(s)

        return add

    def r_m0(s):
        f0, _, _, rd, cs = bufs(s)
        r_wait(f0, R_F0, s)
        add_into(part, (yu, half(s, 0), cs), f0[...])
        r_push(part.at[yu, half(s, 0), cs], rd.at[h0, :], R_D0, s, t_u)

    def r_m1(s):
        _, f1, ru, _, cs = bufs(s)
        r_wait(f1, R_F1, s)
        add_into(part, (yd, half(s, 1), cs), f1[...])
        r_push(part.at[yd, half(s, 1), cs], ru.at[h1, :], R_U1, s, t_d)

    def y_wait(s):
        _, _, ru, rd, _ = bufs(s)
        r_wait(rd.at[h0, :], R_D0, s)
        r_wait(rd.at[h1, :], R_D1, s)
        r_wait(ru.at[h0, :], R_U0, s)
        r_wait(ru.at[h1, :], R_U1, s)

    def y_total(s, cs):
        i = Y_SUMS.index(s)
        return (
            part[y, seg(s), cs].astype(F32)
            + qru[i, :, cs].astype(F32)
            + qrd[i, :, cs].astype(F32)
        )

    def r_y(s):
        y_wait(s)
        part[y, seg(s), col(ox)] = y_total(s, col(ox)).astype(BF)
        r_push(part.at[y, seg(s), col(ox)], qx.at[Y_SUMS.index(s)], R_X, s, t_x)

    def r_end(s):
        if s in Y_SUMS:
            i = Y_SUMS.index(s)
            r_wait(qx.at[i], R_X, s)
            total = y_total(s, col(xl)) + qx[i].astype(F32)
        else:
            i = X_SUMS.index(s)
            r_wait(px.at[i, 3], R_X + 3, s)
            y_wait(s)
            total = (
                part[y, seg(s), col(xl)].astype(F32)
                + px[i, 3].astype(F32)
                + pru[i].astype(F32)
                + prd[i].astype(F32)
            )
        lora = nn_dot(lix[seg(s), :], acat[:, pl.ds(units, feat)])
        outv[seg(s), :] = (total + ADAPTER_SCALE * lora).astype(BF)

    def build_mask():
        lane = lax.broadcasted_iota(jnp.int32, (SEG, WIDE), 1)
        unit = lax.shift_right_logical(lane, 6).astype(F32)
        for s in range(SEGS):
            line = jnp.broadcast_to(slots[pl.ds(s, 1), :].astype(F32), (SEG, SEG))
            wide = jnp.concatenate([line.T] * (WIDE // SEG), axis=1)
            mask[seg(s), :] = jnp.where(wide == unit, 1.0, 0.0).astype(BF)

    def pick(shape, dim, shift):
        i = jnp.bitwise_and(lax.broadcasted_iota(jnp.int32, shape, dim), RANK - 1)
        j = lax.broadcasted_iota(jnp.int32, shape, 1 - dim)
        return jnp.where(i + shift == j, 1.0, 0.0).astype(BF)

    def rank_start():
        ld_c.wait()
        for u in range(USE):
            acat[pl.ds(u * RANK, RANK), :] = aall[lst[0, u]]
        m = mask[...].astype(F32)
        down = (nt_dot(hv[...], acat[:, pl.ds(0, units)]) * m).astype(BF)
        back = (nt_dot(cotf[:, col(me)], acat[:, pl.ds(units, feat)]) * m).astype(BF)
        rk[...] = (
            nn_dot(down, pick((WIDE, 2 * RANK), 0, 0))
            + nn_dot(back, pick((WIDE, 2 * RANK), 0, RANK))
        ).astype(BF)
        push(rk.at[k_col(ox), :], kx, k_ss.at[0, 0], k_rs.at[0, 0], "tp", t_x)

    def k_col(c):
        n = rows_n // 2
        return pl.ds(pl.multiple_of(c * n, 16), n)

    def k_row(t):
        n = rows_n // (2 * NY)
        return pl.ds(pl.multiple_of(t * n, 16), n)

    def rank_x():
        arrived(kx, k_ss.at[0, 0], k_rs.at[0, 0], "tp")
        add_into(rk, (k_col(xl), slice(None)), kx[...])
        for i, t in enumerate((t_u, t_d, t_o)):
            push(rk.at[k_row(t), :], rr.at[i], k_ss.at[1, i], k_rs.at[1, i], "tp", t)

    def rank_sum():
        total = rk[k_row(me), :].astype(F32)
        for i in range(3):
            arrived(rr.at[i], k_ss.at[1, i], k_rs.at[1, i], "tp")
            total = total + rr[i].astype(F32)
        tot[k_row(me), :] = total.astype(BF)
        mine = tot.at[k_row(me), :]
        for i, t in enumerate((t_u, t_d, t_o)):
            push(mine, mine, k_ss.at[2, i], k_rs.at[2, i], "tp", t)

    def rank_y():
        for i, t in enumerate((t_d, t_u, t_o)):
            arrived(tot.at[k_row(t), :], k_ss.at[2, i], k_rs.at[2, i], "tp")
        mine = tot.at[k_col(xl), :]
        push(mine, mine, k_ss.at[0, 1], k_rs.at[0, 1], "tp", t_x)

    def rank_end():
        arrived(tot.at[k_col(ox), :], k_ss.at[0, 1], k_rs.at[0, 1], "tp")
        m = mask[...].astype(F32)
        lix[...] = (nn_dot(tot[...], pick((2 * RANK, WIDE), 1, 0)) * m).astype(BF)
        lbx[...] = (nn_dot(tot[...], pick((2 * RANK, WIDE), 1, RANK)) * m).astype(BF)

    def grads():
        step = 256
        wide = units + feat

        @pl.loop(0, units // step)
        def _(j):
            at = pl.ds(pl.multiple_of(j * step, 128), step)
            ga = tn_dot(lbx[...], hv[:, at]) * grad_scale
            for u in range(USE):
                gslot[u, :, at] = ga[u * RANK : (u + 1) * RANK, :].astype(BF)

        gb = tn_dot(lix[...], cotf[:, col(me)]) * grad_scale
        for u in range(USE):
            gslot[u, :, pl.ds(units, feat)] = gb[u * RANK : (u + 1) * RANK, :].astype(BF)
        gslot[USE] = jnp.zeros((RANK, wide), BF)
        for o in range(4 * NZ):
            at = jnp.int32(USE)
            for u in range(USE):
                at = jnp.where(lst[0, u] == o, u, at)
            con[o % 2, (o // 2) % NZ, o // (2 * NZ)] = gslot[at]

    def s_push(src, dst, slot, dev):
        push(src, dst, s_ss.at[slot], s_rs.at[slot], "grp", dev)

    def s_wait(dst, slot):
        arrived(dst, s_ss.at[slot], s_rs.at[slot], "grp")

    def sum_start():
        for i, zq in enumerate((zo, zu, zd, z)):
            s_push(con.at[1 - core, zq], sb.at[zq], i, n_s)

    def s_o():
        s_wait(sb.at[zo], 0)
        add_into(con, (core, zo), sb[zo])
        s_push(con.at[core, zo, 0], gf.at[0], S_F0, n_u)
        s_push(con.at[core, zo, 1], gf.at[1], S_F1, n_d)

    def s_u():
        s_wait(sb.at[zu], 1)
        add_into(con, (core, zu), sb[zu])
        s_push(con.at[core, zu, 1], grd.at[1], S_D1, n_u)

    def s_d():
        s_wait(sb.at[zd], 2)
        add_into(con, (core, zd), sb[zd])
        s_push(con.at[core, zd, 0], gru.at[0], S_U0, n_d)

    def s_m0():
        s_wait(gf.at[0], S_F0)
        add_into(con, (core, zu, 0), gf[0])
        s_push(con.at[core, zu, 0], grd.at[0], S_D0, n_u)

    def s_m1():
        s_wait(gf.at[1], S_F1)
        add_into(con, (core, zd, 1), gf[1])
        s_push(con.at[core, zd, 1], gru.at[1], S_U1, n_d)

    def sum_total(h):
        return (
            con[core, z, h].astype(F32)
            + sb[z, h].astype(F32)
            + grd[h].astype(F32)
            + gru[h].astype(F32)
        )

    def s_x():
        s_wait(sb.at[z], 3)
        s_wait(grd.at[1], S_D1)
        s_wait(gru.at[0], S_U0)
        s_wait(grd.at[0], S_D0)
        s_wait(gru.at[1], S_U1)
        con[core, z, oxh] = sum_total(oxh).astype(BF)
        s_push(con.at[core, z, oxh], gx, S_X, n_x)

    def s_end():
        s_wait(gx, S_X)
        gtot[...] = sum_total(xh) + gx[...].astype(F32)

    def hidden_tile(part_no):
        rows = pl.ds(0, CUT) if part_no == 0 else pl.ds(CUT, rows_n - CUT)

        def tile(j):
            at = pl.ds(j * 256, 256)
            r = nt_dot(cotf[rows, :], wv[at, :])
            r = r + ADAPTER_SCALE * nn_dot(lbx[rows, :], acat[:, at])
            hv[rows, at] = r.astype(BF)

        return tile

    def sent(n):
        while waited[0] < n:
            sends[waited[0]].wait_send()
            waited[0] += 1

    waited = [0]
    tasks = dict(
        sent=sent,
        gs_x=gs_x,
        gs_u=gs_u,
        gs_d=gs_d,
        g_x=g_x,
        g_d=g_d,
        g_u=g_u,
        g_xd=g_xd,
        g_xu=g_xu,
        g_o0=g_o0,
        g_o1=g_o1,
        g_end=g_end,
        m_start=m_start,
        m_x=m_x,
        m_d=m_d,
        m_u=m_u,
        m_xu=m_xu,
        m_xd=m_xd,
        m_o=m_o,
        m_xo=m_xo,
        m_end=m_end,
        mask=build_mask,
        part=part_block,
        r_so=r_so,
        r_su=r_su,
        r_sd=r_sd,
        r_xo=r_x(0, yo),
        r_xu=r_x(1, yu),
        r_xd=r_x(2, yd),
        r_xm=r_x(3, y),
        r_ao=r_add(0, yo, r_so),
        r_au=r_add(1, yu, r_su),
        r_ad=r_add(2, yd, r_sd),
        r_m0=r_m0,
        r_m1=r_m1,
        r_y=r_y,
        r_end=r_end,
        rank_start=rank_start,
        rank_x=rank_x,
        rank_sum=rank_sum,
        rank_y=rank_y,
        rank_end=rank_end,
        grads=grads,
        sum_start=sum_start,
        s_o=s_o,
        s_u=s_u,
        s_d=s_d,
        s_m0=s_m0,
        s_m1=s_m1,
        s_x=s_x,
        s_end=s_end,
        hidA=hidden_tile(0),
        hidB=hidden_tile(1),
    )
    for name, *index in ORDER:
        tasks[name](*index)
    sent(len(sends))


def fused(hidden, w, cot, amap, bmap, lst, slots, rows_all):
    rows, units = hidden.shape
    feat = cot.shape[1]
    wide = units + feat
    nq, np_ = len(Y_SUMS), len(X_SUMS)
    any_ = pl.BlockSpec(memory_space=pl.ANY)
    dma = pltpu.SemaphoreType.DMA
    v = pltpu.VMEM
    return pl.pallas_call(
        functools.partial(kernel, ADAPTER_SCALE / rows_all),
        out_shape=(
            pltpu.VMEM((rows, feat), BF),
            pltpu.VMEM((rows, units), BF),
            pltpu.VMEM((RANK, wide), F32),
        ),
        in_specs=[any_] * 5
        + [pl.BlockSpec(memory_space=pltpu.SMEM), pl.BlockSpec(memory_space=pltpu.VMEM)],
        out_specs=(pl.BlockSpec(memory_space=pltpu.VMEM),) * 3,
        scratch_shapes=[
            v((units, 2 * NY * feat), BF),
            v((rows, 2 * NY * feat), BF),
            v((NY, rows, 2 * feat), BF),
            v((nq, HALF, 2 * feat), BF),
            v((nq, HALF, 2 * feat), BF),
            v((nq, SEG, 2 * feat), BF),
            v((nq, SEG, 2 * feat), BF),
            v((nq, SEG, feat), BF),
            v((np_, HALF, feat), BF),
            v((np_, HALF, feat), BF),
            v((np_, SEG, feat), BF),
            v((np_, SEG, feat), BF),
            v((np_, NY, SEG, feat), BF),
            v((RANK, units), F32),
            v((RANK, feat), F32),
            v((4 * NZ, RANK, wide), BF),
            v((WIDE, wide), BF),
            v((rows, WIDE), BF),
            v((rows, 2 * RANK), BF),
            v((rows // 2, 2 * RANK), BF),
            v((3, rows // (2 * NY), 2 * RANK), BF),
            v((rows, 2 * RANK), BF),
            v((rows, WIDE), BF),
            v((rows, WIDE), BF),
            v((USE + 1, RANK, wide), BF),
            v((2, NZ, 2, RANK, wide), BF),
            v((NZ, 2, RANK, wide), BF),
            v((2, RANK, wide), BF),
            v((2, RANK, wide), BF),
            v((2, RANK, wide), BF),
            v((RANK, wide), BF),
            dma((4,)),
            dma((2 * NY,)),
            dma((9, SEGS)),
            dma((9, SEGS)),
            dma((10, SEGS)),
            dma((10, SEGS)),
            dma((3, 3)),
            dma((3, 3)),
            dma((7,)),
            dma((7,)),
            dma((8,)),
            dma((8,)),
            dma((11,)),
            dma((11,)),
        ],
        compiler_params=pltpu.CompilerParams(
            collective_id=0,
            has_side_effects=True,
            vmem_limit_bytes=56 * 1024 * 1024,
        ),
    )(hidden, w, cot, amap, bmap, lst, slots)


def finish_kernel(gv, *refs):
    ins, hg_in, out_in = refs[:6], refs[6], refs[7]
    outs, hg_out, out_out = refs[8:14], refs[14], refs[15]
    bufs, st_sem, mv_sem = refs[16:22], refs[22], refs[23]
    moves = [
        pltpu.make_async_copy(hg_in, hg_out, mv_sem.at[0]),
        pltpu.make_async_copy(out_in, out_out, mv_sem.at[1]),
    ]
    for c in moves:
        c.start()
    units, feat = ins[0].shape[1], ins[3].shape[1]
    step = 256
    for n, first, size in ((0, 0, units), (3, units, feat)):
        for j in range(size // step):
            at = pl.ds(j * step, step)
            new = moment_optimizer_step(
                ins[n][:, at], ins[n + 1][:, at], ins[n + 2][:, at], gv[:, pl.ds(first + j * step, step)]
            )
            for i in range(3):
                bufs[n + i][:, at] = new[i]
                c = pltpu.make_async_copy(
                    bufs[n + i].at[:, at], outs[n + i].at[:, at], st_sem.at[n + i, j]
                )
                c.start()
                moves.append(c)
    for c in moves:
        c.wait()


def finish(grad, a, am, av, b, bm, bv, hg, out):
    hbm = pl.BlockSpec(memory_space=pltpu.HBM)
    vm = pl.BlockSpec(memory_space=pltpu.VMEM)
    like = lambda x: jax.ShapeDtypeStruct(x.shape, x.dtype)
    six = (a, am, av, b, bm, bv)
    return pl.pallas_call(
        finish_kernel,
        out_shape=tuple(like(x) for x in six + (hg, out)),
        in_specs=[vm] * 9,
        out_specs=(hbm,) * 8,
        scratch_shapes=[pltpu.VMEM(x.shape, F32) for x in six]
        + [pltpu.SemaphoreType.DMA((6, a.shape[1] // 256)), pltpu.SemaphoreType.DMA((2,))],
        compiler_params=pltpu.CompilerParams(vmem_limit_bytes=8 * 1024 * 1024),
    )(grad, *six, hg, out)


def per_device(
    hidden,
    frozen_down_matrix,
    cotangent,
    adapter_input_maps,
    adapter_output_maps,
    input_first_moment,
    input_second_moment,
    output_first_moment,
    output_second_moment,
    group_adapter_list,
    token_adapter_slot,
):
    rows_all = hidden.shape[0] * lax.axis_size("grp")
    output, hidden_gradient, grad = fused(
        hidden,
        frozen_down_matrix,
        cotangent,
        adapter_input_maps[0],
        adapter_output_maps[0],
        group_adapter_list,
        token_adapter_slot.reshape(SEGS, SEG),
        rows_all,
    )
    new_a, new_a_m, new_a_v, new_b, new_b_m, new_b_v, hidden_gradient, output = finish(
        grad,
        adapter_input_maps[0],
        input_first_moment[0],
        input_second_moment[0],
        adapter_output_maps[0],
        output_first_moment[0],
        output_second_moment[0],
        hidden_gradient,
        output,
    )
    return (
        output,
        hidden_gradient,
        new_a[None],
        new_b[None],
        new_a_m[None],
        new_a_v[None],
        new_b_m[None],
        new_b_v[None],
    )


def solution(mesh):
    return jax.shard_map(
        per_device,
        mesh=mesh,
        in_specs=(
            P("grp", "tp"),
            P("tp", None),
            P("grp", "tp"),
            P("grp", None, "tp"),
            P("grp", None, "tp"),
            P("grp", None, "tp"),
            P("grp", None, "tp"),
            P("grp", None, "tp"),
            P("grp", None, "tp"),
            P("grp", None),
            P("grp"),
        ),
        out_specs=(
            P("grp", "tp"),
            P("grp", "tp"),
            P("grp", None, "tp"),
            P("grp", None, "tp"),
            P("grp", None, "tp"),
            P("grp", None, "tp"),
            P("grp", None, "tp"),
            P("grp", None, "tp"),
        ),
        check_vma=False,
    )
```

```python
import functools

import jax
import jax.numpy as jnp
from jax import lax
from jax.experimental import pallas as pl
from jax.experimental.pallas import tpu as pltpu
from jax.sharding import PartitionSpec as P

MESH = pl.DeviceIdType.MESH
BF = jnp.bfloat16
F32 = jnp.float32

SEG = 128
HALF = 64
SEGS = 7
USE = 4
STEP = 20
RANK = 64
WIDE = USE * RANK
NY = 4
NZ = 4
Y_FIRST = (5, 6)
X_SUMS = (0, 1, 2)
Y_SUMS = tuple(s for s in range(SEGS) if s not in X_SUMS)
CUT = 3 * SEG

ORDER = (
    ("gs_x", 3), ("gs_d", 3), ("gs_u", 4), ("m_start",), ("gs_d", 5),
    ("gs_d", 1), ("gs_u", 2), ("gs_u", 0), ("part", 0), ("gs_x", 4),
    ("g_u", 3), ("part", 1), ("r_xo", 0), ("r_so", 3), ("mask",),
    ("g_u", 5), ("g_d", 4), ("gs_x", 0), ("gs_u", 6), ("gs_d", 6),
    ("m_d",), ("gs_d", 0), ("g_d", 0), ("gs_d", 4), ("r_xo", 2),
    ("m_x",), ("r_so", 4), ("part", 2), ("m_u",), ("part", 3),
    ("r_xu", 0), ("r_su", 5), ("gs_x", 1), ("r_su", 4), ("r_so", 5),
    ("sent", 11), ("m_o",), ("m_xu",), ("part", 4), ("part", 5),
    ("r_sd", 5), ("r_xd", 1), ("gs_x", 6), ("g_x", 4), ("r_xu", 1),
    ("sent", 19), ("m_xd",), ("gs_u", 5), ("gs_u", 3), ("gs_u", 1),
    ("r_sd", 4), ("sent", 26), ("r_m1", 5), ("m_xo",), ("sent", 34),
    ("m_end",), ("rank_start",), ("g_o1", 5), ("g_d", 5), ("g_u", 6),
    ("gs_x", 2), ("g_d", 6), ("r_ad", 1), ("sent", 45), ("rank_x",),
    ("g_x", 0), ("sent", 52), ("g_o1", 6), ("g_x", 3), ("part", 6),
    ("part", 7), ("rank_sum",), ("g_x", 1), ("r_m0", 5), ("g_d", 3),
    ("gs_d", 2), ("g_u", 4), ("g_u", 0), ("sent", 59), ("g_xu", 3),
    ("g_xd", 4), ("g_x", 2), ("g_xd", 3), ("g_xu", 4), ("g_xd", 0),
    ("r_ao", 2), ("g_d", 2), ("r_m1", 3), ("rank_y",), ("g_o0", 6),
    ("g_d", 1), ("g_xd", 1), ("gs_x", 5), ("r_m1", 4), ("r_su", 3),
    ("g_o0", 5), ("r_xd", 2), ("r_au", 0), ("r_au", 1), ("r_m0", 4),
    ("g_xu", 1), ("r_xd", 0), ("r_xu", 2), ("r_xo", 1), ("r_m0", 3),
    ("r_xm", 1), ("g_xu", 0), ("r_sd", 3), ("g_u", 2), ("r_xm", 0),
    ("r_y", 5), ("r_xm", 2), ("g_u", 1), ("rank_end",), ("g_end", 6),
    ("grads",), ("sum_start",), ("g_xd", 2), ("g_end", 5), ("sent", 84),
    ("g_xu", 2), ("g_end", 4), ("g_end", 3), ("hidB", 0), ("s_o",),
    ("hidB", 1), ("r_so", 6), ("r_sd", 6), ("s_d",), ("s_u",),
    ("hidB", 2), ("hidB", 3), ("hidB", 4), ("hidB", 5), ("sent", 101),
    ("s_m0",), ("r_ao", 0), ("s_m1",), ("hidB", 6), ("r_y", 3),
    ("g_end", 0), ("r_y", 4), ("r_ao", 1), ("r_su", 6), ("sent", 111),
    ("g_end", 2), ("r_ad", 2), ("g_end", 1), ("hidA", 0), ("hidA", 1),
    ("hidA", 2), ("r_m1", 6), ("r_m0", 6), ("r_au", 2), ("sent", 118),
    ("s_x",), ("r_end", 3), ("r_m1", 2), ("hidA", 3), ("r_m0", 2),
    ("r_m1", 1), ("r_ad", 0), ("r_m1", 0), ("r_end", 4), ("hidA", 4),
    ("r_end", 5), ("r_m0", 1), ("r_m0", 0), ("sent", 138), ("r_y", 6),
    ("hidA", 5), ("hidA", 6), ("sent", 143), ("r_end", 2), ("r_end", 1),
    ("s_end",), ("r_end", 0), ("r_end", 6),
)

ADAPTER_SCALE = 2.0
LEARN_RATE = 0.001
BETA_ONE = 0.9
BETA_TWO = 0.999
ADAM_EPS = 1e-08


def moment_optimizer_step(param, moment, second, grad):
    new_moment = BETA_ONE * moment + (1.0 - BETA_ONE) * grad
    new_second = BETA_TWO * second + (1.0 - BETA_TWO) * grad * grad
    fix_one = 1.0 - BETA_ONE**STEP
    fix_two = 1.0 - BETA_TWO**STEP
    new_param = param - LEARN_RATE * (new_moment / fix_one) / (
        jnp.sqrt(new_second / fix_two) + ADAM_EPS
    )
    return (new_param, new_moment, new_second)


def nt_dot(a, b):
    return lax.dot_general(a, b, (((1,), (1,)), ((), ())), preferred_element_type=F32)


def tn_dot(a, b):
    return lax.dot_general(a, b, (((0,), (0,)), ((), ())), preferred_element_type=F32)


def nn_dot(a, b):
    return jnp.dot(a, b, preferred_element_type=F32)


G_X, G_U, G_D, G_XU, G_XD, G_O0, G_O1, G_XO0, G_XO1 = range(9)
R_F0, R_F1, R_D0, R_D1, R_U0, R_U1, R_X = range(7)
M_X, M_U, M_D, M_XU, M_XD, M_O, M_XO = range(7)
S_F0, S_F1, S_D0, S_D1, S_U0, S_U1, S_X = range(4, 11)


def kernel(
    grad_scale,
    hid,
    w,
    cot,
    amap,
    bmap,
    lst,
    slots,
    outv,
    hv,
    gtot,
    wv,
    cotf,
    part,
    qf0,
    qf1,
    qru,
    qrd,
    qx,
    pf0,
    pf1,
    pru,
    prd,
    px,
    am32,
    bm32,
    aall,
    acat,
    mask,
    rk,
    kx,
    rr,
    tot,
    lix,
    lbx,
    gslot,
    con,
    sb,
    gf,
    grd,
    gru,
    gx,
    ld_sem,
    w_sem,
    g_ss,
    g_rs,
    r_ss,
    r_rs,
    k_ss,
    k_rs,
    m_ss,
    m_rs,
    b_ss,
    b_rs,
    s_ss,
    s_rs,
):
    feat = cot.shape[1]
    units = hid.shape[1]
    rows_n = hid.shape[0]
    me = lax.axis_index("tp")
    xl, y = lax.div(me, NY), lax.rem(me, NY)
    ox = 1 - xl
    yu, yd, yo = lax.rem(y + 1, NY), lax.rem(y + 3, NY), lax.rem(y + 2, NY)
    t_x, t_u, t_d, t_o = ox * NY + y, xl * NY + yu, xl * NY + yd, xl * NY + yo
    t_xu, t_xd, t_xo = ox * NY + yu, ox * NY + yd, ox * NY + yo
    g = lax.axis_index("grp")
    xh, z, core = lax.div(g, 2 * NZ), lax.rem(lax.div(g, 2), NZ), lax.rem(g, 2)
    zu, zd, zo = lax.rem(z + 1, NZ), lax.rem(z + 3, NZ), lax.rem(z + 2, NZ)
    oxh = 1 - xh

    def grp_id(a, b, c):
        return a * (2 * NZ) + b * 2 + c

    n_x, n_u, n_d = grp_id(oxh, z, core), grp_id(xh, zu, core), grp_id(xh, zd, core)
    n_s = grp_id(xh, z, 1 - core)

    def col(k):
        return pl.ds(pl.multiple_of(k * feat, 128), feat)

    def seg(s):
        return pl.ds(s * SEG, SEG)

    def half(s, h):
        return pl.ds(s * SEG + h * HALF, HALF)

    barrier = pltpu.get_barrier_semaphore()
    for dev in (t_x, t_u, t_d, t_o):
        pl.semaphore_signal(barrier, inc=1, device_id={"tp": dev}, device_id_type=MESH)
    for dev in (n_x, n_u, n_d, n_s):
        pl.semaphore_signal(barrier, inc=1, device_id={"grp": dev}, device_id_type=MESH)

    ld_a = pltpu.make_async_copy(amap, am32, ld_sem.at[0])
    ld_b = pltpu.make_async_copy(bmap, bm32, ld_sem.at[1])
    ld_h = pltpu.make_async_copy(hid, hv, ld_sem.at[2])
    ld_c = pltpu.make_async_copy(cot, cotf.at[:, col(me)], ld_sem.at[3])
    ld_a.start()
    ld_b.start()
    ld_h.start()
    blocks = [(yq, c) for yq in (yo, yu, yd, y) for c in (0, 1)]
    ld_w = []
    for i, (yq, c) in enumerate(blocks):
        k = c * NY + yq
        ld_w.append(pltpu.make_async_copy(w.at[:, col(k)], wv.at[:, col(k)], w_sem.at[i]))
        ld_w[-1].start()
    ld_c.start()

    pl.semaphore_wait(barrier, 8)

    sends = []

    def push(src, dst, ss, rs, axis, dev):
        c = pltpu.make_async_remote_copy(
            src_ref=src,
            dst_ref=dst,
            send_sem=ss,
            recv_sem=rs,
            device_id={axis: dev},
            device_id_type=MESH,
        )
        c.start()
        sends.append(c)

    def arrived(dst, ss, rs, axis):
        pltpu.make_async_remote_copy(
            src_ref=dst,
            dst_ref=dst,
            send_sem=ss,
            recv_sem=rs,
            device_id={axis: me if axis == "tp" else g},
            device_id_type=MESH,
        ).wait_recv()

    def g_push(slot, s, rows, k, dev, src=None):
        ref = cotf.at[rows, col(k)]
        push(ref if src is None else src, ref, g_ss.at[slot, s], g_rs.at[slot, s], "tp", dev)

    def g_wait(slot, s, rows, k):
        arrived(cotf.at[rows, col(k)], g_ss.at[slot, s], g_rs.at[slot, s], "tp")

    def gs_x(s):
        g_push(G_X, s, seg(s), me, t_x, cot.at[seg(s), :])

    def gs_u(s):
        g_push(G_D, s, seg(s), me, t_u, cot.at[seg(s), :])

    def gs_d(s):
        g_push(G_U, s, seg(s), me, t_d, cot.at[seg(s), :])

    def g_x(s):
        g_wait(G_X, s, seg(s), t_x)
        g_push(G_XD, s, seg(s), t_x, t_u)
        g_push(G_XU, s, seg(s), t_x, t_d)

    def g_d(s):
        g_wait(G_D, s, seg(s), t_d)
        g_push(G_O0, s, half(s, 0), t_d, t_u)
        if s in Y_FIRST:
            g_push(G_XD, s, seg(s), t_d, t_x)

    def g_u(s):
        g_wait(G_U, s, seg(s), t_u)
        g_push(G_O1, s, half(s, 1), t_u, t_d)
        if s in Y_FIRST:
            g_push(G_XU, s, seg(s), t_u, t_x)

    def g_xd(s):
        g_wait(G_XD, s, seg(s), t_xd)
        g_push(G_XO0, s, half(s, 0), t_xd, t_u)

    def g_xu(s):
        g_wait(G_XU, s, seg(s), t_xu)
        g_push(G_XO1, s, half(s, 1), t_xu, t_d)

    def g_o0(s):
        g_wait(G_O0, s, half(s, 0), t_o)
        g_push(G_XO0, s, half(s, 0), t_o, t_x)

    def g_o1(s):
        g_wait(G_O1, s, half(s, 1), t_o)
        g_push(G_XO1, s, half(s, 1), t_o, t_x)

    def g_end(s):
        if s in Y_FIRST:
            g_wait(G_X, s, seg(s), t_x)
            g_wait(G_XD, s, seg(s), t_xd)
            g_wait(G_XU, s, seg(s), t_xu)
        else:
            g_wait(G_O0, s, half(s, 0), t_o)
            g_wait(G_O1, s, half(s, 1), t_o)
        g_wait(G_XO0, s, half(s, 0), t_xo)
        g_wait(G_XO1, s, half(s, 1), t_xo)

    def m_push(slot, o, dev):
        push(aall.at[o], aall.at[o], m_ss.at[slot], m_rs.at[slot], "grp", dev)

    def m_wait(slot, o):
        arrived(aall.at[o], m_ss.at[slot], m_rs.at[slot], "grp")

    def b_push(i, o):
        push(aall.at[o], aall.at[o], b_ss.at[i], b_rs.at[i], "grp", n_s)

    def m_start():
        ld_a.wait()
        ld_b.wait()
        aall[g, :, pl.ds(0, units)] = am32[...].astype(BF)
        aall[g, :, pl.ds(units, feat)] = bm32[...].astype(BF)
        m_push(M_X, g, n_x)
        m_push(M_D, g, n_u)
        m_push(M_U, g, n_d)
        b_push(7, g)

    def m_x():
        m_wait(M_X, n_x)
        m_push(M_XD, n_x, n_u)
        m_push(M_XU, n_x, n_d)
        b_push(M_X, n_x)

    def m_d():
        m_wait(M_D, n_d)
        m_push(M_O, n_d, n_u)
        b_push(M_D, n_d)

    def m_u():
        m_wait(M_U, n_u)
        b_push(M_U, n_u)

    def m_xu():
        m_wait(M_XU, grp_id(oxh, zu, core))
        m_push(M_XO, grp_id(oxh, zu, core), n_d)
        b_push(M_XU, grp_id(oxh, zu, core))

    def m_xd():
        m_wait(M_XD, grp_id(oxh, zd, core))
        b_push(M_XD, grp_id(oxh, zd, core))

    def m_o():
        m_wait(M_O, grp_id(xh, zo, core))
        b_push(M_O, grp_id(xh, zo, core))

    def m_xo():
        m_wait(M_XO, grp_id(oxh, zo, core))
        b_push(M_XO, grp_id(oxh, zo, core))

    def m_end():
        sib = 1 - core
        for i, o in (
            (7, grp_id(xh, z, sib)),
            (M_X, grp_id(oxh, z, sib)),
            (M_D, grp_id(xh, zd, sib)),
            (M_U, grp_id(xh, zu, sib)),
            (M_XU, grp_id(oxh, zu, sib)),
            (M_XD, grp_id(oxh, zd, sib)),
            (M_O, grp_id(xh, zo, sib)),
            (M_XO, grp_id(oxh, zo, sib)),
        ):
            arrived(aall.at[o], b_ss.at[i], b_rs.at[i], "grp")

    def part_block(i):
        if i == 0:
            ld_h.wait()
        yq, c = blocks[i]
        k = c * NY + yq
        ld_w[i].wait()
        step = feat // 2

        @pl.loop(0, 2)
        def _(j):
            wt = wv[:, pl.ds(pl.multiple_of(k * feat + j * step, 128), step)]
            at = pl.ds(pl.multiple_of(c * feat + j * step, 128), step)
            part[yq, :, at] = nn_dot(hv[...], wt).astype(BF)

    def r_push(src, dst, slot, s, dev):
        push(src, dst, r_ss.at[slot, s], r_rs.at[slot, s], "tp", dev)

    def r_wait(dst, slot, s):
        arrived(dst, r_ss.at[slot, s], r_rs.at[slot, s], "tp")

    def bufs(s):
        if s in Y_SUMS:
            i = Y_SUMS.index(s)
            return qf0.at[i], qf1.at[i], qru.at[i], qrd.at[i], pl.ds(0, 2 * feat)
        i = X_SUMS.index(s)
        return pf0.at[i], pf1.at[i], pru.at[i], prd.at[i], col(xl)

    h0, h1 = pl.ds(0, HALF), pl.ds(HALF, HALF)

    def add_into(ref, idx, other):
        ref[idx] = (ref[idx].astype(F32) + other.astype(F32)).astype(BF)

    def r_so(s):
        f0, f1, _, _, cs = bufs(s)
        r_push(part.at[yo, half(s, 0), cs], f0, R_F0, s, t_u)
        r_push(part.at[yo, half(s, 1), cs], f1, R_F1, s, t_d)

    def r_su(s):
        _, _, _, rd, cs = bufs(s)
        r_push(part.at[yu, half(s, 1), cs], rd.at[h1, :], R_D1, s, t_u)

    def r_sd(s):
        _, _, ru, _, cs = bufs(s)
        r_push(part.at[yd, half(s, 0), cs], ru.at[h0, :], R_U0, s, t_d)

    def r_x(j, yq):
        def send(s):
            i = X_SUMS.index(s)
            r_push(part.at[yq, seg(s), col(ox)], px.at[i, j], R_X + j, s, t_x)

        return send

    def r_add(j, yq, after):
        def add(s):
            i = X_SUMS.index(s)
            r_wait(px.at[i, j], R_X + j, s)
            add_into(part, (yq, seg(s), col(xl)), px[i, j])
            after(s)

        return add

    def r_m0(s):
        f0, _, _, rd, cs = bufs(s)
        r_wait(f0, R_F0, s)
        add_into(part, (yu, half(s, 0), cs), f0[...])
        r_push(part.at[yu, half(s, 0), cs], rd.at[h0, :], R_D0, s, t_u)

    def r_m1(s):
        _, f1, ru, _, cs = bufs(s)
        r_wait(f1, R_F1, s)
        add_into(part, (yd, half(s, 1), cs), f1[...])
        r_push(part.at[yd, half(s, 1), cs], ru.at[h1, :], R_U1, s, t_d)

    def y_wait(s):
        _, _, ru, rd, _ = bufs(s)
        r_wait(rd.at[h0, :], R_D0, s)
        r_wait(rd.at[h1, :], R_D1, s)
        r_wait(ru.at[h0, :], R_U0, s)
        r_wait(ru.at[h1, :], R_U1, s)

    def y_total(s, cs):
        i = Y_SUMS.index(s)
        return (
            part[y, seg(s), cs].astype(F32)
            + qru[i, :, cs].astype(F32)
            + qrd[i, :, cs].astype(F32)
        )

    def r_y(s):
        y_wait(s)
        part[y, seg(s), col(ox)] = y_total(s, col(ox)).astype(BF)
        r_push(part.at[y, seg(s), col(ox)], qx.at[Y_SUMS.index(s)], R_X, s, t_x)

    def r_end(s):
        if s in Y_SUMS:
            i = Y_SUMS.index(s)
            r_wait(qx.at[i], R_X, s)
            total = y_total(s, col(xl)) + qx[i].astype(F32)
        else:
            i = X_SUMS.index(s)
            r_wait(px.at[i, 3], R_X + 3, s)
            y_wait(s)
            total = (
                part[y, seg(s), col(xl)].astype(F32)
                + px[i, 3].astype(F32)
                + pru[i].astype(F32)
                + prd[i].astype(F32)
            )
        lora = nn_dot(lix[seg(s), :], acat[:, pl.ds(units, feat)])
        outv[seg(s), :] = (total + ADAPTER_SCALE * lora).astype(BF)

    def build_mask():
        lane = lax.broadcasted_iota(jnp.int32, (SEG, WIDE), 1)
        unit = lax.shift_right_logical(lane, 6).astype(F32)
        for s in range(SEGS):
            line = jnp.broadcast_to(slots[pl.ds(s, 1), :].astype(F32), (SEG, SEG))
            wide = jnp.concatenate([line.T] * (WIDE // SEG), axis=1)
            mask[seg(s), :] = jnp.where(wide == unit, 1.0, 0.0).astype(BF)

    def pick(shape, dim, shift):
        i = jnp.bitwise_and(lax.broadcasted_iota(jnp.int32, shape, dim), RANK - 1)
        j = lax.broadcasted_iota(jnp.int32, shape, 1 - dim)
        return jnp.where(i + shift == j, 1.0, 0.0).astype(BF)

    def rank_start():
        ld_c.wait()
        for u in range(USE):
            acat[pl.ds(u * RANK, RANK), :] = aall[lst[0, u]]
        m = mask[...].astype(F32)
        down = (nt_dot(hv[...], acat[:, pl.ds(0, units)]) * m).astype(BF)
        back = (nt_dot(cotf[:, col(me)], acat[:, pl.ds(units, feat)]) * m).astype(BF)
        rk[...] = (
            nn_dot(down, pick((WIDE, 2 * RANK), 0, 0))
            + nn_dot(back, pick((WIDE, 2 * RANK), 0, RANK))
        ).astype(BF)
        push(rk.at[k_col(ox), :], kx, k_ss.at[0, 0], k_rs.at[0, 0], "tp", t_x)

    def k_col(c):
        n = rows_n // 2
        return pl.ds(pl.multiple_of(c * n, 16), n)

    def k_row(t):
        n = rows_n // (2 * NY)
        return pl.ds(pl.multiple_of(t * n, 16), n)

    def rank_x():
        arrived(kx, k_ss.at[0, 0], k_rs.at[0, 0], "tp")
        add_into(rk, (k_col(xl), slice(None)), kx[...])
        for i, t in enumerate((t_u, t_d, t_o)):
            push(rk.at[k_row(t), :], rr.at[i], k_ss.at[1, i], k_rs.at[1, i], "tp", t)

    def rank_sum():
        total = rk[k_row(me), :].astype(F32)
        for i in range(3):
            arrived(rr.at[i], k_ss.at[1, i], k_rs.at[1, i], "tp")
            total = total + rr[i].astype(F32)
        tot[k_row(me), :] = total.astype(BF)
        mine = tot.at[k_row(me), :]
        for i, t in enumerate((t_u, t_d, t_o)):
            push(mine, mine, k_ss.at[2, i], k_rs.at[2, i], "tp", t)

    def rank_y():
        for i, t in enumerate((t_d, t_u, t_o)):
            arrived(tot.at[k_row(t), :], k_ss.at[2, i], k_rs.at[2, i], "tp")
        mine = tot.at[k_col(xl), :]
        push(mine, mine, k_ss.at[0, 1], k_rs.at[0, 1], "tp", t_x)

    def rank_end():
        arrived(tot.at[k_col(ox), :], k_ss.at[0, 1], k_rs.at[0, 1], "tp")
        m = mask[...].astype(F32)
        lix[...] = (nn_dot(tot[...], pick((2 * RANK, WIDE), 1, 0)) * m).astype(BF)
        lbx[...] = (nn_dot(tot[...], pick((2 * RANK, WIDE), 1, RANK)) * m).astype(BF)

    def grads():
        step = 256
        wide = units + feat

        @pl.loop(0, units // step)
        def _(j):
            at = pl.ds(pl.multiple_of(j * step, 128), step)
            ga = tn_dot(lbx[...], hv[:, at]) * grad_scale
            for u in range(USE):
                gslot[u, :, at] = ga[u * RANK : (u + 1) * RANK, :].astype(BF)

        gb = tn_dot(lix[...], cotf[:, col(me)]) * grad_scale
        for u in range(USE):
            gslot[u, :, pl.ds(units, feat)] = gb[u * RANK : (u + 1) * RANK, :].astype(BF)
        gslot[USE] = jnp.zeros((RANK, wide), BF)
        for o in range(4 * NZ):
            at = jnp.int32(USE)
            for u in range(USE):
                at = jnp.where(lst[0, u] == o, u, at)
            con[o % 2, (o // 2) % NZ, o // (2 * NZ)] = gslot[at]

    def s_push(src, dst, slot, dev):
        push(src, dst, s_ss.at[slot], s_rs.at[slot], "grp", dev)

    def s_wait(dst, slot):
        arrived(dst, s_ss.at[slot], s_rs.at[slot], "grp")

    def sum_start():
        for i, zq in enumerate((zo, zu, zd, z)):
            s_push(con.at[1 - core, zq], sb.at[zq], i, n_s)

    def s_o():
        s_wait(sb.at[zo], 0)
        add_into(con, (core, zo), sb[zo])
        s_push(con.at[core, zo, 0], gf.at[0], S_F0, n_u)
        s_push(con.at[core, zo, 1], gf.at[1], S_F1, n_d)

    def s_u():
        s_wait(sb.at[zu], 1)
        add_into(con, (core, zu), sb[zu])
        s_push(con.at[core, zu, 1], grd.at[1], S_D1, n_u)

    def s_d():
        s_wait(sb.at[zd], 2)
        add_into(con, (core, zd), sb[zd])
        s_push(con.at[core, zd, 0], gru.at[0], S_U0, n_d)

    def s_m0():
        s_wait(gf.at[0], S_F0)
        add_into(con, (core, zu, 0), gf[0])
        s_push(con.at[core, zu, 0], grd.at[0], S_D0, n_u)

    def s_m1():
        s_wait(gf.at[1], S_F1)
        add_into(con, (core, zd, 1), gf[1])
        s_push(con.at[core, zd, 1], gru.at[1], S_U1, n_d)

    def sum_total(h):
        return (
            con[core, z, h].astype(F32)
            + sb[z, h].astype(F32)
            + grd[h].astype(F32)
            + gru[h].astype(F32)
        )

    def s_x():
        s_wait(sb.at[z], 3)
        s_wait(grd.at[1], S_D1)
        s_wait(gru.at[0], S_U0)
        s_wait(grd.at[0], S_D0)
        s_wait(gru.at[1], S_U1)
        con[core, z, oxh] = sum_total(oxh).astype(BF)
        s_push(con.at[core, z, oxh], gx, S_X, n_x)

    def s_end():
        s_wait(gx, S_X)
        gtot[...] = sum_total(xh) + gx[...].astype(F32)

    def hidden_tile(part_no):
        rows = pl.ds(0, CUT) if part_no == 0 else pl.ds(CUT, rows_n - CUT)

        def tile(j):
            at = pl.ds(j * 256, 256)
            r = nt_dot(cotf[rows, :], wv[at, :])
            r = r + ADAPTER_SCALE * nn_dot(lbx[rows, :], acat[:, at])
            hv[rows, at] = r.astype(BF)

        return tile

    def sent(n):
        while waited[0] < n:
            sends[waited[0]].wait_send()
            waited[0] += 1

    waited = [0]
    tasks = dict(
        sent=sent,
        gs_x=gs_x,
        gs_u=gs_u,
        gs_d=gs_d,
        g_x=g_x,
        g_d=g_d,
        g_u=g_u,
        g_xd=g_xd,
        g_xu=g_xu,
        g_o0=g_o0,
        g_o1=g_o1,
        g_end=g_end,
        m_start=m_start,
        m_x=m_x,
        m_d=m_d,
        m_u=m_u,
        m_xu=m_xu,
        m_xd=m_xd,
        m_o=m_o,
        m_xo=m_xo,
        m_end=m_end,
        mask=build_mask,
        part=part_block,
        r_so=r_so,
        r_su=r_su,
        r_sd=r_sd,
        r_xo=r_x(0, yo),
        r_xu=r_x(1, yu),
        r_xd=r_x(2, yd),
        r_xm=r_x(3, y),
        r_ao=r_add(0, yo, r_so),
        r_au=r_add(1, yu, r_su),
        r_ad=r_add(2, yd, r_sd),
        r_m0=r_m0,
        r_m1=r_m1,
        r_y=r_y,
        r_end=r_end,
        rank_start=rank_start,
        rank_x=rank_x,
        rank_sum=rank_sum,
        rank_y=rank_y,
        rank_end=rank_end,
        grads=grads,
        sum_start=sum_start,
        s_o=s_o,
        s_u=s_u,
        s_d=s_d,
        s_m0=s_m0,
        s_m1=s_m1,
        s_x=s_x,
        s_end=s_end,
        hidA=hidden_tile(0),
        hidB=hidden_tile(1),
    )
    for name, *index in ORDER:
        tasks[name](*index)
    sent(len(sends))


def fused(hidden, w, cot, amap, bmap, lst, slots, rows_all):
    rows, units = hidden.shape
    feat = cot.shape[1]
    wide = units + feat
    nq, np_ = len(Y_SUMS), len(X_SUMS)
    any_ = pl.BlockSpec(memory_space=pl.ANY)
    dma = pltpu.SemaphoreType.DMA
    v = pltpu.VMEM
    return pl.pallas_call(
        functools.partial(kernel, ADAPTER_SCALE / rows_all),
        out_shape=(
            pltpu.VMEM((rows, feat), BF),
            pltpu.VMEM((rows, units), BF),
            pltpu.VMEM((RANK, wide), F32),
        ),
        in_specs=[any_] * 5
        + [pl.BlockSpec(memory_space=pltpu.SMEM), pl.BlockSpec(memory_space=pltpu.VMEM)],
        out_specs=(pl.BlockSpec(memory_space=pltpu.VMEM),) * 3,
        scratch_shapes=[
            v((units, 2 * NY * feat), BF),
            v((rows, 2 * NY * feat), BF),
            v((NY, rows, 2 * feat), BF),
            v((nq, HALF, 2 * feat), BF),
            v((nq, HALF, 2 * feat), BF),
            v((nq, SEG, 2 * feat), BF),
            v((nq, SEG, 2 * feat), BF),
            v((nq, SEG, feat), BF),
            v((np_, HALF, feat), BF),
            v((np_, HALF, feat), BF),
            v((np_, SEG, feat), BF),
            v((np_, SEG, feat), BF),
            v((np_, NY, SEG, feat), BF),
            v((RANK, units), F32),
            v((RANK, feat), F32),
            v((4 * NZ, RANK, wide), BF),
            v((WIDE, wide), BF),
            v((rows, WIDE), BF),
            v((rows, 2 * RANK), BF),
            v((rows // 2, 2 * RANK), BF),
            v((3, rows // (2 * NY), 2 * RANK), BF),
            v((rows, 2 * RANK), BF),
            v((rows, WIDE), BF),
            v((rows, WIDE), BF),
            v((USE + 1, RANK, wide), BF),
            v((2, NZ, 2, RANK, wide), BF),
            v((NZ, 2, RANK, wide), BF),
            v((2, RANK, wide), BF),
            v((2, RANK, wide), BF),
            v((2, RANK, wide), BF),
            v((RANK, wide), BF),
            dma((4,)),
            dma((2 * NY,)),
            dma((9, SEGS)),
            dma((9, SEGS)),
            dma((10, SEGS)),
            dma((10, SEGS)),
            dma((3, 3)),
            dma((3, 3)),
            dma((7,)),
            dma((7,)),
            dma((8,)),
            dma((8,)),
            dma((11,)),
            dma((11,)),
        ],
        compiler_params=pltpu.CompilerParams(
            collective_id=0,
            has_side_effects=True,
            vmem_limit_bytes=56 * 1024 * 1024,
        ),
    )(hidden, w, cot, amap, bmap, lst, slots)


def finish_kernel(gv, *refs):
    ins, hg_in, out_in = refs[:6], refs[6], refs[7]
    outs, hg_out, out_out = refs[8:14], refs[14], refs[15]
    bufs, st_sem, mv_sem = refs[16:22], refs[22], refs[23]
    moves = [
        pltpu.make_async_copy(hg_in, hg_out, mv_sem.at[0]),
        pltpu.make_async_copy(out_in, out_out, mv_sem.at[1]),
    ]
    for c in moves:
        c.start()
    units, feat = ins[0].shape[1], ins[3].shape[1]
    step = 256
    for n, first, size in ((0, 0, units), (3, units, feat)):
        for j in range(size // step):
            at = pl.ds(j * step, step)
            new = moment_optimizer_step(
                ins[n][:, at], ins[n + 1][:, at], ins[n + 2][:, at], gv[:, pl.ds(first + j * step, step)]
            )
            for i in range(3):
                bufs[n + i][:, at] = new[i]
                c = pltpu.make_async_copy(
                    bufs[n + i].at[:, at], outs[n + i].at[:, at], st_sem.at[n + i, j]
                )
                c.start()
                moves.append(c)
    for c in moves:
        c.wait()


def finish(grad, a, am, av, b, bm, bv, hg, out):
    hbm = pl.BlockSpec(memory_space=pltpu.HBM)
    vm = pl.BlockSpec(memory_space=pltpu.VMEM)
    like = lambda x: jax.ShapeDtypeStruct(x.shape, x.dtype)
    six = (a, am, av, b, bm, bv)
    return pl.pallas_call(
        finish_kernel,
        out_shape=tuple(like(x) for x in six + (hg, out)),
        in_specs=[vm] * 9,
        out_specs=(hbm,) * 8,
        scratch_shapes=[pltpu.VMEM(x.shape, F32) for x in six]
        + [pltpu.SemaphoreType.DMA((6, a.shape[1] // 256)), pltpu.SemaphoreType.DMA((2,))],
        compiler_params=pltpu.CompilerParams(vmem_limit_bytes=8 * 1024 * 1024),
    )(grad, *six, hg, out)


def per_device(
    hidden,
    frozen_down_matrix,
    cotangent,
    adapter_input_maps,
    adapter_output_maps,
    input_first_moment,
    input_second_moment,
    output_first_moment,
    output_second_moment,
    group_adapter_list,
    token_adapter_slot,
):
    rows_all = hidden.shape[0] * lax.axis_size("grp")
    output, hidden_gradient, grad = fused(
        hidden,
        frozen_down_matrix,
        cotangent,
        adapter_input_maps[0],
        adapter_output_maps[0],
        group_adapter_list,
        token_adapter_slot.reshape(SEGS, SEG),
        rows_all,
    )
    new_a, new_a_m, new_a_v, new_b, new_b_m, new_b_v, hidden_gradient, output = finish(
        grad,
        adapter_input_maps[0],
        input_first_moment[0],
        input_second_moment[0],
        adapter_output_maps[0],
        output_first_moment[0],
        output_second_moment[0],
        hidden_gradient,
        output,
    )
    return (
        output,
        hidden_gradient,
        new_a[None],
        new_b[None],
        new_a_m[None],
        new_a_v[None],
        new_b_m[None],
        new_b_v[None],
    )


def solution(mesh):
    return jax.shard_map(
        per_device,
        mesh=mesh,
        in_specs=(
            P("grp", "tp"),
            P("tp", None),
            P("grp", "tp"),
            P("grp", None, "tp"),
            P("grp", None, "tp"),
            P("grp", None, "tp"),
            P("grp", None, "tp"),
            P("grp", None, "tp"),
            P("grp", None, "tp"),
            P("grp", None),
            P("grp"),
        ),
        out_specs=(
            P("grp", "tp"),
            P("grp", "tp"),
            P("grp", None, "tp"),
            P("grp", None, "tp"),
            P("grp", None, "tp"),
            P("grp", None, "tp"),
            P("grp", None, "tp"),
            P("grp", None, "tp"),
        ),
        check_vma=False,
    )
```
